256 devices in a mesh: row: 8 (over z), col: 32 (over y, x, core).
Axes of the slice: x: 4, y: 4, z: 8, core: 2. Of those that a mesh axis runs over, the one named last changes fastest.
Arguments:
- tile_u: bfloat16 [1024, 64, 256], P('col', 'row'), may hold values from -6 to 6
- tile_v: bfloat16 [1024, 64, 256], P('col', 'row'), may hold values from -0.1875 to 0.1875
- inverse_factor: bfloat16 [1024, 1024], P('row', 'col'), as said below
- ranks: int32 [64], P('row'), may hold values from 16 to 256, as said below
- panel_index: int32 [1], replicated, may hold values from -32 to 61
Outputs:
- trailing_right: bfloat16 [64, 64, 1024, 256], P('row', 'col')
- panel_solved: bfloat16 [1024, 64, 256], P('col', 'row')
The draws below stay inside these ranges and needn't reach their ends.
Inputs may be any that keep to these rules, and one draw needn't show every extreme that they name: `ranks`: each rank is a multiple of 16; in every draw some tile has rank 256 and some has rank 16. `inverse_factor`: lower triangular with a positive diagonal.
All inputs are finite; a program needn't handle non-finite values.
Results may differ from the reference program's by a relative error of at most 0.006.
Values may be sent and summed in bfloat16 or wider, within the bound.
A program may use at most 128 MiB of HBM per device.

```python
import jax
import jax.numpy as jnp
from jax import lax

B = 1024
RMAX = 256
TC = 2
TR = 8
NTR = 64
NCT = 64
N_ROW = 8
N_COL = 32


def draw_inverse_factor(key, part):
    key = jax.random.fold_in(key, 11)
    diag_key, off_key = jax.random.split(key, 2)
    rows_at = jnp.arange(B, dtype=jnp.int32)[:, None]
    cols_at = jnp.arange(B, dtype=jnp.int32)[None, :]
    lower = (cols_at < rows_at).astype(jnp.float32)
    diagonal = (cols_at == rows_at).astype(jnp.float32)
    entries = jax.random.normal(off_key, (B, B), jnp.float32)
    diag_values = jax.random.uniform(diag_key, (B, 1), jnp.float32, 0.6, 1.4)
    matrix = lower * entries * (1.0 / B ** 0.5) + diagonal * diag_values
    return matrix.astype(jnp.bfloat16)


def draw_ranks(key, part):
    key = jax.random.fold_in(key, 23)
    base_key, high_key, low_key = jax.random.split(key, 3)
    values = 16 * jax.random.randint(base_key, (NTR,), 1, RMAX // 16 + 1)
    high_at = jax.random.randint(high_key, (), 0, NTR)
    low_at = (high_at + jax.random.randint(low_key, (), 1, NTR)) % NTR
    values = values.at[high_at].set(RMAX)
    values = values.at[low_at].set(16)
    return values.astype(jnp.int32)


def levels(rng, extent, pieces, low, largest):
    level = 1.0
    for axis_at, shards_of in pieces:
        heights = jax.random.uniform(jax.random.fold_in(jax.random.fold_in(rng, 6), axis_at), (shards_of,), jnp.float32, low / len(pieces), largest / len(pieces))
        level = level * jnp.repeat(jnp.exp(heights), extent[axis_at] // shards_of).reshape((-1,) + (1,) * (len(extent) - 1 - axis_at))
    return level


def noise(rng, dims, deviation, bound, pieces=(), kind=jnp.bfloat16):
    drawn = deviation * jax.random.normal(rng, dims, jnp.float32)
    if pieces:
        drawn = drawn * levels(rng, dims, pieces, -0.22, 0.18)
    return jnp.clip(drawn, -bound, bound).astype(kind)


def setup_inputs(seed: int = 0) -> dict:
    arg_keys = jax.random.split(jax.random.key(seed), 6)
    tile_u = noise(arg_keys[0], (B, NTR, RMAX), 1.0, 6.0, ((0, 32), (1, 8)))
    tile_v = noise(arg_keys[1], (B, NTR, RMAX), B ** -0.5, 0.1875, ((0, 32), (1, 8)))
    inverse_factor = draw_inverse_factor(jax.random.fold_in(arg_keys[5], 71), 0)
    ranks = draw_ranks(jax.random.fold_in(arg_keys[5], 71), 0)
    panel_index = jax.random.randint(arg_keys[4], (1,), 0 - NCT // 2, NCT - 2).astype(jnp.int32)
    return {"tile_u": tile_u, "tile_v": tile_v, "inverse_factor": inverse_factor, "ranks": ranks, "panel_index": panel_index}


def reference(tile_u, tile_v, inverse_factor, ranks, panel_index):
    panel_at = panel_index[0]
    index_rows = jnp.arange(NTR, dtype=jnp.int32)
    index_cols = jnp.arange(NCT, dtype=jnp.int32)
    row_tile = (index_rows % TR) * N_ROW + index_rows // TR
    col_tile = (index_cols % TC) * N_COL + index_cols // TC
    rank_mask = (jnp.arange(RMAX, dtype=jnp.int32)[None, :] < ranks[:, None]) & (row_tile[:, None] > panel_at)
    masked_v = tile_v * rank_mask[None, :, :].astype(jnp.bfloat16)
    solved = jnp.dot(inverse_factor, masked_v.reshape(B, NTR * RMAX), preferred_element_type=jnp.float32)
    panel_solved = solved.astype(jnp.bfloat16).reshape(B, NTR, RMAX)
    source_index = (col_tile % N_ROW) * TR + col_tile // N_ROW
    column_u = jnp.take(tile_u, source_index, axis=1).astype(jnp.float32)
    column_v = jnp.take(panel_solved, source_index, axis=1).astype(jnp.float32)

    def one_row(row_index):
        own_solved = lax.dynamic_index_in_dim(panel_solved, row_index, 1, keepdims=False).astype(jnp.float32)
        core_blocks = jnp.einsum("btr,bs->trs", column_v, own_solved).astype(jnp.bfloat16)
        core_blocks = lax.optimization_barrier(core_blocks).astype(jnp.float32)
        product = jnp.einsum("btr,trs->tbs", column_u, core_blocks)
        live_mask = (col_tile > panel_at) & (col_tile <= row_tile[row_index])
        return (product * live_mask[:, None, None].astype(jnp.float32)).astype(jnp.bfloat16)

    trailing_right = lax.map(one_row, index_rows)
    return trailing_right, panel_solved
```

```python
import jax
import jax.numpy as jnp
from jax import lax
from jax.experimental import pallas as pl
from jax.experimental.pallas import tpu as pltpu
from jax.sharding import PartitionSpec as P

MESH = pl.DeviceIdType.MESH
NZ = 8
NX = 4
NY = 4
VW = 512
PW = 768


def dev(r, c):
    return (r, c)


def gather_kernel(
    js_ref, lt_ref, x_out, j_out, xg, jg,
    sc_s, sc_r, l_s, l_r, near_s, near_r, far_s, far_r, sib_s, sib_r, z_s, z_r,
    out_sem,
):
    r = lax.axis_index("row")
    c = lax.axis_index("col")
    y = lax.div(c, 8)
    x = lax.rem(lax.div(c, 2), 4)
    k = lax.rem(c, 2)
    sib = c + 1 - 2 * k
    home = lax.rem(c, 8)
    spread = lax.div(c, 4)
    itself = jnp.logical_and(spread == r, home == r)
    xp = y * 8 + lax.rem(x + 1, 4) * 2 + k
    xm = y * 8 + lax.rem(x + 3, 4) * 2 + k
    yp = lax.rem(y + 1, 4) * 8 + x * 2 + k
    ym = lax.rem(y + 3, 4) * 8 + x * 2 + k

    barrier = pltpu.get_barrier_semaphore()

    def hello(rr, cc):
        pl.semaphore_signal(barrier, inc=1, device_id=(rr, cc), device_id_type=MESH)

    for i in range(1, NZ):
        hello(lax.rem(r + i, NZ), c)
    for cc in (xp, xm, yp, ym, sib):
        hello(r, cc)
    for i in range(4):
        cc = 4 * r + i

        @pl.when(jnp.logical_not(jnp.logical_and(home == r, cc == c)))
        def _():
            hello(home, cc)

    for q in range(4):
        for t in range(2):
            s = 4 * t + q
            at = PW * (s // 2) + 256 * (s % 2)
            xg[y, x, k, :, at : at + 256] = js_ref[q, 0, t]
    l_at = pl.multiple_of(lax.div(r, 2) * PW + VW + lax.rem(r, 2) * 128, 128)
    xg[y, x, k, :, pl.ds(l_at, 128)] = lt_ref[...]

    @pl.when(itself)
    def _():
        pl.semaphore_wait(barrier, 15)

    @pl.when(jnp.logical_not(itself))
    def _():
        pl.semaphore_wait(barrier, 16)

    def scatter(q, w):
        return pltpu.make_async_remote_copy(
            src_ref=js_ref.at[q, w],
            dst_ref=jg.at[:, w, pl.ds(pl.multiple_of(c * 32, 32), 32)],
            send_sem=sc_s.at[w, q],
            recv_sem=sc_r.at[w, lax.rem(c, 4)],
            device_id=(spread, 8 * q + r),
            device_id_type=MESH,
        )

    def linv(i):
        return pltpu.make_async_remote_copy(
            src_ref=xg.at[y, x, k, :, pl.ds(l_at, 128)],
            dst_ref=xg.at[y, x, k, :, pl.ds(l_at, 128)],
            send_sem=l_s.at[i - 1],
            recv_sem=l_r.at[i - 1],
            device_id=(lax.rem(r + i, NZ), c),
            device_id_type=MESH,
        )

    def not_me(q):
        return jnp.logical_not(jnp.logical_and(spread == r, 8 * q + r == c))

    first_x = (True, True, False, False)
    long_way = (1, -1, 1, -1)
    VCOLS, LCOLS, ALL = (0, VW), (VW, PW - VW), (0, PW)

    def step_of(p, m):
        if m == 2:
            return (-1, 1) if long_way[p] == 1 else (1, -1)
        return (0, 1) if m == 0 else (0, -1)

    def near(p, m, part):
        off, way = step_of(p, m)
        cols = pl.ds(PW * p + part[0], part[1])
        if first_x[p]:
            ref = xg.at[y, lax.rem(x + 4 + off, 4), k, :, cols]
            to = xp if way == 1 else xm
        else:
            ref = xg.at[lax.rem(y + 4 + off, 4), x, k, :, cols]
            to = yp if way == 1 else ym
        kind = 0 if part is VCOLS else 1
        return pltpu.make_async_remote_copy(
            src_ref=ref, dst_ref=ref,
            send_sem=near_s.at[kind, p, m], recv_sem=near_r.at[kind, p, m],
            device_id=(r, to), device_id_type=MESH,
        )

    def group(p, off):
        cols = pl.ds(PW * p, PW)
        if first_x[p]:
            return xg.at[lax.rem(y + 4 + off, 4), :, k, :, cols]
        return xg.at[:, lax.rem(x + 4 + off, 4), k, :, cols]

    def far(p, m):
        off, way = step_of(p, m)
        ref = group(p, off)
        if first_x[p]:
            to = yp if way == 1 else ym
        else:
            to = xp if way == 1 else xm
        return pltpu.make_async_remote_copy(
            src_ref=ref, dst_ref=ref,
            send_sem=far_s.at[p, m], recv_sem=far_r.at[p, m],
            device_id=(r, to), device_id_type=MESH,
        )

    def sibling(p, off):
        ref = group(p, off)
        return pltpu.make_async_remote_copy(
            src_ref=ref, dst_ref=ref,
            send_sem=sib_s.at[p, off + 1], recv_sem=sib_r.at[p, off + 1],
            device_id=(r, sib), device_id_type=MESH,
        )

    def reach(t, d):
        return 4 if t == d else 3

    def along_z(w, t, d, s):
        way = 1 if d == 0 else NZ - 1
        block = lax.rem(r + s * (NZ - way), NZ)
        ref = jg.at[t, w, pl.ds(pl.multiple_of(block * 128, 128), 128)]
        return pltpu.make_async_remote_copy(
            src_ref=ref, dst_ref=ref,
            send_sem=z_s.at[w, t, d, s], recv_sem=z_r.at[w, t, d, s],
            device_id=(lax.rem(r + way, NZ), c), device_id_type=MESH,
        )

    def z_event(w, s):
        for t in range(2):
            for d in range(2):
                if 0 < s <= reach(t, d):
                    along_z(w, t, d, s - 1).wait_recv()
                if s < reach(t, d):
                    along_z(w, t, d, s).start()

    def scattered(w):
        for i in range(4):

            @pl.when(jnp.logical_not(jnp.logical_and(home == r, 4 * r + i == c)))
            def _():
                pltpu.make_async_remote_copy(
                    src_ref=js_ref.at[0, w],
                    dst_ref=jg.at[:, w, pl.ds(pl.multiple_of((4 * r + i) * 32, 32), 32)],
                    send_sem=sc_s.at[w, 0],
                    recv_sem=sc_r.at[w, i],
                    device_id=(home, 4 * r + i),
                    device_id_type=MESH,
                ).wait_recv()

    def scatter_event(w):
        for q in range(4):

            @pl.when(not_me(q))
            def _():
                scatter(q, w).start()

            @pl.when(jnp.logical_not(not_me(q)))
            def _():
                jg[:, w, pl.ds(pl.multiple_of(c * 32, 32), 32)] = js_ref[q, w]

    for i in (4, 3, 5, 2, 6, 1, 7):
        linv(i).start()
    scatter_event(0)
    for p in range(4):
        near(p, 0, VCOLS).start()
        near(p, 1, VCOLS).start()
    scatter_event(1)
    for i in range(1, NZ):
        linv(i).wait_recv()
    for p in range(4):
        near(p, 0, LCOLS).start()
        near(p, 1, LCOLS).start()
    scattered(0)
    z_event(0, 0)
    scattered(1)
    z_event(1, 0)

    def onward(p):
        return 0 if long_way[p] == 1 else 1

    for part in (VCOLS, LCOLS):
        for p in range(4):
            near(p, onward(p), part).wait_recv()
            near(p, 2, part).start()
    for p in range(4):
        for part in (VCOLS, LCOLS):
            near(p, 1 - onward(p), part).wait_recv()
            near(p, 2, part).wait_recv()
        far(p, 0).start()
        far(p, 1).start()
        sibling(p, 0).start()
    z_event(0, 1)
    z_event(1, 1)
    z_event(0, 2)
    z_event(1, 2)
    for p in range(4):
        far(p, onward(p)).wait_recv()
        far(p, 2).start()
        sibling(p, -long_way[p]).start()
    z_event(0, 3)
    for p in range(4):
        far(p, 1 - onward(p)).wait_recv()
        sibling(p, long_way[p]).start()
    z_event(1, 3)
    z_event(0, 4)
    for p in range(4):
        far(p, 2).wait_recv()
        sibling(p, 2).start()
    z_event(1, 4)
    out_j = pltpu.make_async_copy(jg, j_out, out_sem.at[1])
    out_j.start()
    for off in (0, 1, -1, 2):
        for p in range(4):
            sibling(p, off).wait_recv()

    out_x = pltpu.make_async_copy(xg, x_out, out_sem.at[0])
    out_x.start()

    for i in range(1, NZ):
        linv(i).wait_send()
    for w in range(2):
        for q in range(4):

            @pl.when(not_me(q))
            def _():
                scatter(q, w).wait_send()

        for t in range(2):
            for d in range(2):
                for s in range(reach(t, d)):
                    along_z(w, t, d, s).wait_send()
    for p in range(4):
        for m in range(3):
            near(p, m, VCOLS).wait_send()
            near(p, m, LCOLS).wait_send()
            far(p, m).wait_send()
        for off in range(-1, 3):
            sibling(p, off).wait_send()
    out_x.wait()
    out_j.wait()


def gather(js, lt):
    dma = pltpu.SemaphoreType.DMA
    return pl.pallas_call(
        gather_kernel,
        out_shape=(
            jax.ShapeDtypeStruct((NY, NX, 2, 32, 4 * PW), jnp.bfloat16),
            jax.ShapeDtypeStruct((2, 2, 1024, 256), jnp.bfloat16),
        ),
        in_specs=[pl.BlockSpec(memory_space=pltpu.VMEM)] * 2,
        out_specs=[pl.BlockSpec(memory_space=pl.ANY)] * 2,
        scratch_shapes=[
            pltpu.VMEM((NY, NX, 2, 32, 4 * PW), jnp.bfloat16),
            pltpu.VMEM((2, 2, 1024, 256), jnp.bfloat16),
            dma((2, 4)), dma((2, 4)),
            dma((7,)), dma((7,)),
            dma((2, 4, 3)), dma((2, 4, 3)),
            dma((4, 3)), dma((4, 3)),
            dma((4, 4)), dma((4, 4)),
            dma((2, 2, 2, 4)), dma((2, 2, 2, 4)),
            dma((2,)),
        ],
        compiler_params=pltpu.CompilerParams(
            collective_id=0, has_side_effects=True, vmem_limit_bytes=48 * 2**20
        ),
        name="gather",
    )(js, lt)


def update_kernel(
    k_ref, v_ref, l0, l1, l2, l3, j_ref, out_ref, solved_ref, linv, sjt, sa
):
    a = pl.program_id(0)
    r = lax.axis_index("row")
    c = lax.axis_index("col")

    def solve(v, write):
        for m in range(4):
            depth = 256 * (m + 1)
            block = jnp.dot(
                linv[256 * m : 256 * m + 256, :depth], v[:depth, :],
                preferred_element_type=jnp.float32,
            ).astype(jnp.bfloat16)
            write(m, block)

    @pl.when(a == 0)
    def _():
        for m, piece in enumerate((l0, l1, l2, l3)):
            for n in range(m + 1):
                linv[256 * m : 256 * m + 256, 256 * n : 256 * n + 256] = piece[
                    256 * n : 256 * n + 256, :
                ].T
        for t in range(2):
            def put(m, block):
                sjt[t, :, 256 * m : 256 * m + 256] = block.T

            solve(j_ref.at[t, 0], put)

    def keep(m, block):
        sa[256 * m : 256 * m + 256, :] = block

    solve(v_ref, keep)
    solved_ref[...] = sa[pl.ds(pl.multiple_of(c * 32, 32), 32), :]
    row_tile = a * NZ + r
    for t in range(2):
        col_tile = c + 32 * t
        live = jnp.logical_and(col_tile > k_ref[0], col_tile <= row_tile)

        @pl.when(live)
        def _():
            core = jnp.dot(
                sjt[t], sa[...], preferred_element_type=jnp.float32
            ).astype(jnp.bfloat16)
            for m in range(4):
                out_ref[0, t, 256 * m : 256 * m + 256, :] = jnp.dot(
                    j_ref[t, 1, 256 * m : 256 * m + 256, :], core,
                    preferred_element_type=jnp.float32,
                ).astype(jnp.bfloat16)

        @pl.when(jnp.logical_not(live))
        def _():
            out_ref[0, t] = jnp.zeros((1024, 256), jnp.bfloat16)


def update(panel_index, xs, jg):
    def column(at):
        return pl.BlockSpec((1024, 256), lambda a, at=at: (0, at))

    return pl.pallas_call(
        update_kernel,
        grid=(8,),
        out_shape=(
            jax.ShapeDtypeStruct((8, 2, 1024, 256), jnp.bfloat16),
            jax.ShapeDtypeStruct((32, 2048), jnp.bfloat16),
        ),
        in_specs=[
            pl.BlockSpec(memory_space=pltpu.SMEM),
            pl.BlockSpec((1024, 256), lambda a: (0, 3 * (a // 2) + a % 2)),
            column(2), column(5), column(8), column(11),
            pl.BlockSpec((2, 2, 1024, 256), lambda a: (0, 0, 0, 0)),
        ],
        out_specs=[
            pl.BlockSpec((1, 2, 1024, 256), lambda a: (a, 0, 0, 0)),
            pl.BlockSpec((32, 256), lambda a: (0, a)),
        ],
        scratch_shapes=[
            pltpu.VMEM((1024, 1024), jnp.bfloat16),
            pltpu.VMEM((2, 256, 1024), jnp.bfloat16),
            pltpu.VMEM((1024, 256), jnp.bfloat16),
        ],
        compiler_params=pltpu.CompilerParams(
            dimension_semantics=("arbitrary",), vmem_limit_bytes=48 * 2**20
        ),
        name="update",
    )(panel_index, xs, xs, xs, xs, xs, jg)


def per_device(tile_u, tile_v, inverse_factor, ranks, panel_index):
    row_place = lax.axis_index("row")
    rows, slots, width = tile_v.shape
    row_tile = jnp.arange(slots, dtype=jnp.int32) * NZ + row_place
    rank_mask = (jnp.arange(width, dtype=jnp.int32)[None, :] < ranks[:, None]) & (
        row_tile[:, None] > panel_index[0]
    )
    masked_v = tile_v * rank_mask[None, :, :].astype(jnp.bfloat16)

    def by_target(tiles):
        return tiles.reshape(rows, 2, 4, width).transpose(2, 1, 0, 3)

    js = jnp.stack([by_target(masked_v), by_target(tile_u)], axis=1)
    xg, jg = gather(js, inverse_factor.T)
    out, solved = update(panel_index, xg.reshape(1024, 4 * PW), jg)
    return out, solved.reshape(rows, slots, width)


def solution(mesh):
    placed = (P("col", "row", None), P("col", "row", None), P("row", "col"), P("row"), P())
    return jax.shard_map(
        per_device,
        mesh=mesh,
        in_specs=placed,
        out_specs=(P("row", "col", None, None), P("col", "row", None)),
        check_vma=False,
    )
```

```python
import jax
import jax.numpy as jnp
from jax import lax
from jax.experimental import pallas as pl
from jax.experimental.pallas import tpu as pltpu
from jax.sharding import PartitionSpec as P

MESH = pl.DeviceIdType.MESH
NZ = 8
NX = 4
NY = 4
VW = 512
LW = 256


def dev(r, c):
    return (r, c)


def gather_kernel(
    rank_ref, k_ref, u_hbm, v_hbm, lt_hbm, core_out, u_out, solved_out,
    u_ref, v_ref, js, vg, lg, jg, linv, sjt, sa, core,
    sc_s, sc_r, l_s, l_r, near_s, near_r, far_s, far_r, sib_s, sib_r, z_s, z_r,
    v_s, out_sem,
):
    r = lax.axis_index("row")
    c = lax.axis_index("col")
    y = lax.div(c, 8)
    x = lax.rem(lax.div(c, 2), 4)
    k = lax.rem(c, 2)
    sib = c + 1 - 2 * k
    home = lax.rem(c, 8)
    spread = lax.div(c, 4)
    itself = jnp.logical_and(spread == r, home == r)
    xp = y * 8 + lax.rem(x + 1, 4) * 2 + k
    xm = y * 8 + lax.rem(x + 3, 4) * 2 + k
    yp = lax.rem(y + 1, 4) * 8 + x * 2 + k
    ym = lax.rem(y + 3, 4) * 8 + x * 2 + k

    def when(cond, act):
        if cond is True:
            act()
        else:
            pl.when(cond)(act)

    l_at = pl.multiple_of(r * 128, 128)
    loads = (
        pltpu.make_async_copy(v_hbm, v_ref, out_sem.at[0]),
        pltpu.make_async_copy(lt_hbm, lg.at[y, x, k, :, pl.ds(l_at, 128)], out_sem.at[1]),
        pltpu.make_async_copy(u_hbm, u_ref, out_sem.at[2]),
    )
    for load in loads:
        load.start()
    barrier = pltpu.get_barrier_semaphore()

    def hello(rr, cc):
        pl.semaphore_signal(barrier, inc=1, device_id=(rr, cc), device_id_type=MESH)

    for i in range(1, NZ):
        hello(lax.rem(r + i, NZ), c)
    for cc in (xp, xm, yp, ym, sib):
        hello(r, cc)
    for i in range(4):
        cc = 4 * r + i
        when(
            jnp.logical_not(jnp.logical_and(home == r, cc == c)),
            lambda cc=cc: hello(home, cc),
        )

    for load in loads:
        load.wait()
    lane = lax.broadcasted_iota(jnp.int32, (32, 256), 1)
    by_slot = jnp.swapaxes(v_ref[...], 0, 1)
    for s in range(8):
        width = jnp.where(s * NZ + r > k_ref[0], rank_ref[s], 0)
        kept = by_slot[s] * (lane < width).astype(jnp.bfloat16)
        js[s % 4, 0, s // 4] = kept
        vg[y, x, k, :, 256 * s : 256 * s + 256] = kept
    by_slot = jnp.swapaxes(u_ref[...], 0, 1)
    for s in range(8):
        js[s % 4, 1, s // 4] = by_slot[s]

    @pl.when(itself)
    def _():
        pl.semaphore_wait(barrier, 15)

    @pl.when(jnp.logical_not(itself))
    def _():
        pl.semaphore_wait(barrier, 16)

    def scatter(q, w):
        return pltpu.make_async_remote_copy(
            src_ref=js.at[q, w],
            dst_ref=jg.at[:, w, pl.ds(pl.multiple_of(c * 32, 32), 32)],
            send_sem=sc_s.at[w, q],
            recv_sem=sc_r.at[w, lax.rem(c, 4)],
            device_id=(spread, 8 * q + r),
            device_id_type=MESH,
        )

    def not_me(q):
        return jnp.logical_not(jnp.logical_and(spread == r, 8 * q + r == c))

    def scatter_event(w):
        for q in range(4):
            when(not_me(q), lambda: scatter(q, w).start())

            @pl.when(jnp.logical_not(not_me(q)))
            def _():
                jg[:, w, pl.ds(pl.multiple_of(c * 32, 32), 32)] = js[q, w]

    def scattered(w):
        for i in range(4):

            @pl.when(jnp.logical_not(jnp.logical_and(home == r, 4 * r + i == c)))
            def _():
                pltpu.make_async_remote_copy(
                    src_ref=js.at[0, w],
                    dst_ref=jg.at[:, w, pl.ds(pl.multiple_of((4 * r + i) * 32, 32), 32)],
                    send_sem=sc_s.at[w, 0],
                    recv_sem=sc_r.at[w, i],
                    device_id=(home, 4 * r + i),
                    device_id_type=MESH,
                ).wait_recv()

    def linv_copy(i):
        return pltpu.make_async_remote_copy(
            src_ref=lg.at[y, x, k, :, pl.ds(l_at, 128)],
            dst_ref=lg.at[y, x, k, :, pl.ds(l_at, 128)],
            send_sem=l_s.at[i - 1],
            recv_sem=l_r.at[i - 1],
            device_id=(lax.rem(r + i, NZ), c),
            device_id_type=MESH,
        )

    V, L = 0, 1
    first_x = (True, True, False, False)
    long_way = (1, -1, 1, -1)
    came = (-1, 1, 2)

    def step_of(p, m):
        if m == 2:
            return (-1, 1) if long_way[p] == 1 else (1, -1)
        return (0, 1) if m == 0 else (0, -1)

    def at(pos, off):
        return lax.rem(pos + 4 + off, 4)

    def columns(kind, p):
        return pl.ds(VW * p, VW) if kind == V else pl.ds(LW * p, LW)

    def near_live(kind, p, off):
        if kind == V or p == 3:
            return True
        return (y if first_x[p] else at(y, off)) <= p

    def far_live(kind, p, off):
        if kind == V or p == 3 or not first_x[p]:
            return True
        return at(y, off) <= p

    def near(kind, p, m):
        off, way = step_of(p, m)
        buf = vg if kind == V else lg
        cols = columns(kind, p)
        if first_x[p]:
            ref = buf.at[y, at(x, off), k, :, cols]
            to = xp if way == 1 else xm
        else:
            ref = buf.at[at(y, off), x, k, :, cols]
            to = yp if way == 1 else ym
        return pltpu.make_async_remote_copy(
            src_ref=ref, dst_ref=ref,
            send_sem=v_s.at[0] if kind == V else near_s.at[p, m],
            recv_sem=near_r.at[kind, p, m],
            device_id=(r, to), device_id_type=MESH,
        )

    def group(kind, p, off):
        cols = columns(kind, p)
        if kind == V:
            if first_x[p]:
                return vg.at[at(y, off), :, k, :, cols]
            return vg.at[:, at(x, off), k, :, cols]
        if first_x[p]:
            return lg.at[at(y, off), :, k, :, cols]
        return lg.at[pl.ds(0, p + 1), at(x, off), k, :, cols]

    def far(kind, p, m):
        off, way = step_of(p, m)
        ref = group(kind, p, off)
        if first_x[p]:
            to = yp if way == 1 else ym
        else:
            to = xp if way == 1 else xm
        return pltpu.make_async_remote_copy(
            src_ref=ref, dst_ref=ref,
            send_sem=v_s.at[1] if kind == V else far_s.at[p, m],
            recv_sem=far_r.at[kind, p, m],
            device_id=(r, to), device_id_type=MESH,
        )

    def sibling(kind, p, off):
        ref = group(kind, p, off)
        return pltpu.make_async_remote_copy(
            src_ref=ref, dst_ref=ref,
            send_sem=v_s.at[2] if kind == V else sib_s.at[p, off + 1],
            recv_sem=sib_r.at[kind, p, off + 1 if kind == L else 0],
            device_id=(r, sib), device_id_type=MESH,
        )

    def onward(p):
        return 0 if long_way[p] == 1 else 1

    def near_start(kind, p, m):
        when(near_live(kind, p, step_of(p, m)[0]), lambda: near(kind, p, m).start())

    def near_got(kind, p, m):
        when(near_live(kind, p, came[m]), lambda: near(kind, p, m).wait_recv())

    def far_start(kind, p, m):
        when(far_live(kind, p, step_of(p, m)[0]), lambda: far(kind, p, m).start())

    def far_got(kind, p, m):
        when(far_live(kind, p, came[m]), lambda: far(kind, p, m).wait_recv())

    def sib_start(kind, p, off):
        when(far_live(kind, p, off), lambda: sibling(kind, p, off).start())

    def sib_got(kind, p):
        if kind == V:
            ref = vg.at[:, :, 1 - k, :, columns(V, p)]
            pltpu.make_async_remote_copy(
                src_ref=ref, dst_ref=ref, send_sem=v_s.at[2],
                recv_sem=sib_r.at[V, p, 0],
                device_id=(r, sib), device_id_type=MESH,
            ).wait_recv()
            return
        for off in (0, 1, -1, 2):
            when(far_live(kind, p, off), lambda: sibling(kind, p, off).wait_recv())

    def near_first(kind):
        for p in range(4):
            near_start(kind, p, 0)
            near_start(kind, p, 1)

    def near_second(kind):
        for p in range(4):
            near_got(kind, p, onward(p))
            near_start(kind, p, 2)

    def far_first(kind, pieces):
        for p in pieces:
            near_got(kind, p, 1 - onward(p))
            near_got(kind, p, 2)
            far_start(kind, p, 0)
            far_start(kind, p, 1)
            sib_start(kind, p, 0)

    def far_second(kind, pieces):
        for p in pieces:
            far_got(kind, p, onward(p))
            far_start(kind, p, 2)
            sib_start(kind, p, came[onward(p)])

    def far_third(kind, pieces):
        for p in pieces:
            far_got(kind, p, 1 - onward(p))
            sib_start(kind, p, came[1 - onward(p)])

    def far_last(kind, pieces):
        for p in pieces:
            far_got(kind, p, 2)
            sib_start(kind, p, 2)

    def reach(t, d):
        return 4 if t == d else 3

    def along_z(w, t, d, s):
        way = 1 if d == 0 else NZ - 1
        block = lax.rem(r + s * (NZ - way), NZ)
        ref = jg.at[t, w, pl.ds(pl.multiple_of(block * 128, 128), 128)]
        return pltpu.make_async_remote_copy(
            src_ref=ref, dst_ref=ref,
            send_sem=z_s, recv_sem=z_r.at[w, t, d, s],
            device_id=(lax.rem(r + way, NZ), c), device_id_type=MESH,
        )

    def z_event(w, s):
        for t in range(2):
            for d in range(2):
                if 0 < s <= reach(t, d):
                    along_z(w, t, d, s - 1).wait_recv()
                if s < reach(t, d):
                    along_z(w, t, d, s).start()

    def solve(load, put):
        for m in range(4):
            total = None
            for n in range(m + 1):
                part = jnp.dot(
                    linv[256 * m : 256 * m + 256, 256 * n : 256 * n + 256], load(n),
                    preferred_element_type=jnp.float32,
                )
                total = part if total is None else total + part
            put(m, total.astype(jnp.bfloat16))

    def factor_turned():
        for m in range(4):
            for n in range(m + 1):
                linv[256 * m : 256 * m + 256, 256 * n : 256 * n + 256] = lg[
                    n, :, :, :, 256 * m : 256 * m + 256
                ].reshape(256, 256).T

    def columns_solved():
        def tile(t, carry):
            def put(m, block):
                sjt[t, :, 256 * m : 256 * m + 256] = block.T

            solve(lambda n: jg[t, 0, 256 * n : 256 * n + 256, :], put)
            return carry

        lax.fori_loop(0, 2, tile, 0)

    def slots(p):
        def slot(i, carry):
            s = 2 * p + i
            cols = pl.ds(pl.multiple_of(s * 256, 256), 256)

            def put(m, block):
                sa[256 * m : 256 * m + 256, :] = block

            solve(lambda n: vg[n, :, :, :, cols].reshape(256, 256), put)
            solved_out[s] = sa[pl.ds(pl.multiple_of(c * 32, 32), 32), :]
            for t in range(2):

                @pl.when(c + 32 * t <= s * NZ + r)
                def _():
                    core[s, t] = jnp.dot(
                        sjt[t], sa[...], preferred_element_type=jnp.float32
                    ).astype(jnp.bfloat16)

            return carry

        lax.fori_loop(0, 2, slot, 0)

    for i in (4, 3, 5, 2, 6, 1, 7):
        when(y <= lax.div(r, 2), lambda: linv_copy(i).start())
    scatter_event(0)
    near_first(V)
    scatter_event(1)
    for i in range(1, NZ):
        when(
            y <= lax.div(lax.rem(r + NZ - i, NZ), 2),
            lambda: linv_copy(i).wait_recv(),
        )
    near_first(L)
    scattered(0)
    z_event(0, 0)
    near_second(V)
    near_second(L)
    scattered(1)
    z_event(1, 0)
    far_first(L, range(4))
    far_first(V, (0, 2))
    z_event(0, 1)
    far_second(L, range(4))
    z_event(1, 1)
    far_second(V, (0, 2))
    far_first(V, (1, 3))
    far_third(L, range(4))
    far_last(L, range(4))
    z_event(0, 2)
    z_event(1, 2)
    far_third(V, (0, 2))
    far_second(V, (1, 3))
    for p in range(4):
        sib_got(L, p)
    factor_turned()
    z_event(0, 3)
    z_event(1, 3)
    far_last(V, (0, 2))
    far_third(V, (1, 3))
    z_event(0, 4)
    columns_solved()
    sib_got(V, 0)
    slots(0)
    far_last(V, (1, 3))
    sib_got(V, 2)
    slots(2)
    sib_got(V, 1)
    slots(1)
    sib_got(V, 3)
    slots(3)
    out_core = pltpu.make_async_copy(core, core_out, out_sem.at[0])
    out_core.start()
    z_event(1, 4)
    out_u = pltpu.make_async_copy(jg.at[:, 1], u_out, out_sem.at[1])
    out_u.start()

    for sem, rows in ((v_s.at[0], 192), (v_s.at[1], 768), (v_s.at[2], 1024), (z_s, 896)):
        ref = linv.at[pl.ds(0, rows)]
        pltpu.make_async_remote_copy(
            src_ref=ref, dst_ref=ref, send_sem=sem, recv_sem=l_r.at[0],
            device_id=(r, sib), device_id_type=MESH,
        ).wait_send()
    for i in range(1, NZ):
        when(y <= lax.div(r, 2), lambda: linv_copy(i).wait_send())
    for w in range(2):
        for q in range(4):
            when(not_me(q), lambda: scatter(q, w).wait_send())
    for p in range(4):
        for m in range(3):
            off = step_of(p, m)[0]
            when(near_live(L, p, off), lambda: near(L, p, m).wait_send())
            when(far_live(L, p, off), lambda: far(L, p, m).wait_send())
        for off in range(-1, 3):
            when(far_live(L, p, off), lambda: sibling(L, p, off).wait_send())
    out_core.wait()
    out_u.wait()


def gather(ranks, panel_index, tile_u, tile_v, inverse_factor):
    dma = pltpu.SemaphoreType.DMA
    bf16 = jnp.bfloat16
    vmem = pl.BlockSpec(memory_space=pltpu.VMEM)
    smem = pl.BlockSpec(memory_space=pltpu.SMEM)
    hbm = pl.BlockSpec(memory_space=pl.ANY)
    return pl.pallas_call(
        gather_kernel,
        out_shape=(
            jax.ShapeDtypeStruct((8, 2, 256, 256), bf16),
            jax.ShapeDtypeStruct((2, 1024, 256), bf16),
            jax.ShapeDtypeStruct((8, 32, 256), bf16),
        ),
        in_specs=[smem, smem, hbm, hbm, hbm],
        out_specs=[hbm, hbm, vmem],
        scratch_shapes=[
            pltpu.VMEM((32, 8, 256), bf16),
            pltpu.VMEM((32, 8, 256), bf16),
            pltpu.VMEM((4, 2, 2, 32, 256), bf16),
            pltpu.VMEM((NY, NX, 2, 32, 4 * VW), bf16),
            pltpu.VMEM((NY, NX, 2, 32, 4 * LW), bf16),
            pltpu.VMEM((2, 2, 1024, 256), bf16),
            pltpu.VMEM((1024, 1024), bf16),
            pltpu.VMEM((2, 256, 1024), bf16),
            pltpu.VMEM((1024, 256), bf16),
            pltpu.VMEM((8, 2, 256, 256), bf16),
            dma((2, 4)), dma((2, 4)),
            dma((7,)), dma((7,)),
            dma((4, 3)), dma((2, 4, 3)),
            dma((4, 3)), dma((2, 4, 3)),
            dma((4, 4)), dma((2, 4, 4)),
            dma, dma((2, 2, 2, 4)),
            dma((3,)), dma((3,)),
        ],
        compiler_params=pltpu.CompilerParams(
            collective_id=0, has_side_effects=True, vmem_limit_bytes=60 * 2**20
        ),
        name="gather",
    )(ranks, panel_index, tile_u, tile_v, inverse_factor)


def update_kernel(k_ref, core_ref, u_ref, solved_ref, out_ref, solved_out):
    a = pl.program_id(0)

    @pl.when(a == 0)
    def _():
        solved_out[...] = jnp.swapaxes(solved_ref[...], 0, 1)

    row_tile = a * NZ + lax.axis_index("row")
    for t in range(2):
        col_tile = lax.axis_index("col") + 32 * t
        live = jnp.logical_and(col_tile > k_ref[0], col_tile <= row_tile)

        @pl.when(live)
        def _():
            for m in range(4):
                out_ref[0, t, 256 * m : 256 * m + 256, :] = jnp.dot(
                    u_ref[t, 256 * m : 256 * m + 256, :], core_ref[0, t],
                    preferred_element_type=jnp.float32,
                ).astype(jnp.bfloat16)

        @pl.when(jnp.logical_not(live))
        def _():
            out_ref[0, t] = jnp.zeros((1024, 256), jnp.bfloat16)


def update(panel_index, core, column_u, solved):
    return pl.pallas_call(
        update_kernel,
        grid=(8,),
        out_shape=(
            jax.ShapeDtypeStruct((8, 2, 1024, 256), jnp.bfloat16),
            jax.ShapeDtypeStruct((32, 8, 256), jnp.bfloat16),
        ),
        in_specs=[
            pl.BlockSpec(memory_space=pltpu.SMEM),
            pl.BlockSpec((1, 2, 256, 256), lambda a: (a, 0, 0, 0)),
            pl.BlockSpec((2, 1024, 256), lambda a: (0, 0, 0)),
            pl.BlockSpec((8, 32, 256), lambda a: (0, 0, 0)),
        ],
        out_specs=[
            pl.BlockSpec((1, 2, 1024, 256), lambda a: (a, 0, 0, 0)),
            pl.BlockSpec((32, 8, 256), lambda a: (0, 0, 0)),
        ],
        compiler_params=pltpu.CompilerParams(
            dimension_semantics=("arbitrary",), vmem_limit_bytes=60 * 2**20
        ),
        name="update",
    )(panel_index, core, column_u, solved)


def per_device(tile_u, tile_v, inverse_factor, ranks, panel_index):
    core, column_u, solved = gather(ranks, panel_index, tile_u, tile_v, inverse_factor.T)
    return update(panel_index, core, column_u, solved)


def solution(mesh):
    placed = (P("col", "row", None), P("col", "row", None), P("row", "col"), P("row"), P())
    return jax.shard_map(
        per_device,
        mesh=mesh,
        in_specs=placed,
        out_specs=(P("row", "col", None, None), P("col", "row", None)),
        check_vma=False,
    )
```

```python
import jax
import jax.numpy as jnp
from jax import lax
from jax.experimental import pallas as pl
from jax.experimental.pallas import tpu as pltpu
from jax.sharding import PartitionSpec as P

MESH = pl.DeviceIdType.MESH
NZ = 8
NX = 4
NY = 4
VW = 1024
LW = 512


def dev(r, c):
    return (r, c)


def gather_kernel(
    rank_ref, k_ref, u_hbm, v_hbm, lt_hbm, core_out, u_out, solved_out,
    u_ref, v_ref, js, vg, lg, jg, linv, sjt, sa, core,
    sc_s, sc_r, l_s, l_r, near_r, far_r, sib_r, z_s, z_r, v_s, out_sem,
):
    r = lax.axis_index("row")
    c = lax.axis_index("col")
    y = lax.div(c, 8)
    x = lax.rem(lax.div(c, 2), 4)
    k = lax.rem(c, 2)
    sib = c + 1 - 2 * k
    home = lax.rem(c, 8)
    spread = lax.div(c, 4)
    itself = jnp.logical_and(spread == r, home == r)
    xp = y * 8 + lax.rem(x + 1, 4) * 2 + k
    xm = y * 8 + lax.rem(x + 3, 4) * 2 + k
    yp = lax.rem(y + 1, 4) * 8 + x * 2 + k
    ym = lax.rem(y + 3, 4) * 8 + x * 2 + k
    xx = y * 8 + lax.rem(x + 2, 4) * 2 + k
    yy = lax.rem(y + 2, 4) * 8 + x * 2 + k

    def when(cond, act):
        if cond is True:
            act()
        else:
            pl.when(cond)(act)

    l_at = pl.multiple_of(r * 128, 128)
    loads = (
        pltpu.make_async_copy(v_hbm, v_ref, out_sem.at[0]),
        pltpu.make_async_copy(lt_hbm, lg.at[y, x, k, :, pl.ds(l_at, 128)], out_sem.at[1]),
        pltpu.make_async_copy(u_hbm, u_ref, out_sem.at[2]),
    )
    for load in loads:
        load.start()
    barrier = pltpu.get_barrier_semaphore()

    def hello(rr, cc):
        pl.semaphore_signal(barrier, inc=1, device_id=(rr, cc), device_id_type=MESH)

    for i in range(1, NZ):
        hello(lax.rem(r + i, NZ), c)
    for cc in (xp, xm, xx, yp, ym, yy, sib):
        hello(r, cc)
    for i in range(4):
        cc = 4 * r + i
        when(
            jnp.logical_not(jnp.logical_and(home == r, cc == c)),
            lambda cc=cc: hello(home, cc),
        )

    for load in loads:
        load.wait()
    lane = lax.broadcasted_iota(jnp.int32, (32, 256), 1)
    by_slot = jnp.swapaxes(v_ref[...], 0, 1)
    for s in range(8):
        width = jnp.where(s * NZ + r > k_ref[0], rank_ref[s], 0)
        kept = by_slot[s] * (lane < width).astype(jnp.bfloat16)
        js[s % 4, 0, s // 4] = kept
        vg[y, x, k, :, 256 * s : 256 * s + 256] = kept
    by_slot = jnp.swapaxes(u_ref[...], 0, 1)
    for s in range(8):
        js[s % 4, 1, s // 4] = by_slot[s]

    @pl.when(itself)
    def _():
        pl.semaphore_wait(barrier, 17)

    @pl.when(jnp.logical_not(itself))
    def _():
        pl.semaphore_wait(barrier, 18)

    def scatter(q, w):
        return pltpu.make_async_remote_copy(
            src_ref=js.at[q, w],
            dst_ref=jg.at[:, w, pl.ds(pl.multiple_of(c * 32, 32), 32)],
            send_sem=sc_s.at[w, q],
            recv_sem=sc_r.at[w, lax.rem(c, 4)],
            device_id=(spread, 8 * q + r),
            device_id_type=MESH,
        )

    def not_me(q):
        return jnp.logical_not(jnp.logical_and(spread == r, 8 * q + r == c))

    def scatter_event(w):
        for q in range(4):
            when(not_me(q), lambda: scatter(q, w).start())

            @pl.when(jnp.logical_not(not_me(q)))
            def _():
                jg[:, w, pl.ds(pl.multiple_of(c * 32, 32), 32)] = js[q, w]

    def scattered(w):
        for i in range(4):

            @pl.when(jnp.logical_not(jnp.logical_and(home == r, 4 * r + i == c)))
            def _():
                pltpu.make_async_remote_copy(
                    src_ref=js.at[0, w],
                    dst_ref=jg.at[:, w, pl.ds(pl.multiple_of((4 * r + i) * 32, 32), 32)],
                    send_sem=sc_s.at[w, 0],
                    recv_sem=sc_r.at[w, i],
                    device_id=(home, 4 * r + i),
                    device_id_type=MESH,
                ).wait_recv()

    def linv_copy(i):
        return pltpu.make_async_remote_copy(
            src_ref=lg.at[y, x, k, :, pl.ds(l_at, 128)],
            dst_ref=lg.at[y, x, k, :, pl.ds(l_at, 128)],
            send_sem=l_s.at[i - 1],
            recv_sem=l_r.at[i - 1],
            device_id=(lax.rem(r + i, NZ), c),
            device_id_type=MESH,
        )

    def linv_live(rr):
        return jnp.logical_or(y < 2, rr >= 4)

    V, L = 0, 1
    came = (-1, 1, 2)

    def at(pos, off):
        return lax.rem(pos + 4 + off, 4)

    def columns(kind, p, half=None):
        width = VW if kind == V else LW
        first = width * (p if kind == V else 1 - p)
        if half is not None:
            width //= 2
            first += width * half
        return pl.ds(first, width)

    def near_live(kind, p, off):
        if kind == V or p == 0:
            return True
        return at(y, off) < 2

    def near(kind, p, m, off=0):
        buf = vg if kind == V else lg
        cols = columns(kind, p)
        if p == 0:
            ref = buf.at[y, at(x, off), k, :, cols]
            to = (xp, xm, xx)[m]
        else:
            ref = buf.at[at(y, off), x, k, :, cols]
            to = (yp, ym, yy)[m]
        return pltpu.make_async_remote_copy(
            src_ref=ref, dst_ref=ref,
            send_sem=v_s.at[4 if kind == L and p == 1 else 3 if kind == L else 0],
            recv_sem=near_r.at[kind, p, m],
            device_id=(r, to), device_id_type=MESH,
        )

    def group(kind, p, off, half=None):
        cols = columns(kind, p, half)
        if kind == V:
            if p == 0:
                return vg.at[at(y, off), :, k, :, cols]
            return vg.at[:, at(x, off), k, :, cols]
        if p == 0:
            return lg.at[at(y, off), :, k, :, cols]
        return lg.at[pl.ds(0, 2), at(x, off), k, :, cols]

    def far(kind, p, m):
        if m < 2:
            ref = group(kind, p, 0)
        else:
            ref = group(kind, p, came[m - 2], m - 2)
        if p == 0:
            to = ym if m % 2 else yp
        else:
            to = xm if m % 2 else xp
        return pltpu.make_async_remote_copy(
            src_ref=ref, dst_ref=ref,
            send_sem=v_s.at[1 if kind == V else 3], recv_sem=far_r.at[kind, p, m],
            device_id=(r, to), device_id_type=MESH,
        )

    def sibling(kind, p, off):
        ref = group(kind, p, off)
        return pltpu.make_async_remote_copy(
            src_ref=ref, dst_ref=ref,
            send_sem=v_s.at[2 if kind == V else 3], recv_sem=sib_r.at[kind, p],
            device_id=(r, sib), device_id_type=MESH,
        )

    def near_start(kind, p):
        for m in (2, 0, 1):
            near(kind, p, m).start()

    def far_start(kind, p):
        for m in range(3):
            when(
                near_live(kind, p, came[m]),
                lambda: near(kind, p, m, came[m]).wait_recv(),
            )
        far(kind, p, 0).start()
        far(kind, p, 1).start()
        sibling(kind, p, 0).start()

    def far_more(kind, p, m):
        far(kind, p, m).wait_recv()
        far(kind, p, m + 2).start()
        sibling(kind, p, came[m]).start()

    def far_end(kind, p):
        far(kind, p, 2).wait_recv()
        far(kind, p, 3).wait_recv()
        sibling(kind, p, 2).start()

    def sib_got(kind, p):
        cols = columns(kind, p)
        if kind == V:
            ref = vg.at[:, :, 1 - k, :, cols]
        elif p == 0:
            ref = lg.at[:, :, 1 - k, :, cols]
        else:
            ref = lg.at[pl.ds(0, 2), :, 1 - k, :, cols]
        pltpu.make_async_remote_copy(
            src_ref=ref, dst_ref=ref, send_sem=v_s.at[2], recv_sem=sib_r.at[kind, p],
            device_id=(r, sib), device_id_type=MESH,
        ).wait_recv()

    def along_z(w, d, s):
        way = 1 if d == 0 else NZ - 1
        block = lax.rem(r + s * (NZ - way), NZ)
        rows = pl.ds(pl.multiple_of(block * 128, 128), 128)
        ref = jg.at[:, w, rows] if s < 3 else jg.at[d, w, rows]
        return pltpu.make_async_remote_copy(
            src_ref=ref, dst_ref=ref,
            send_sem=z_s, recv_sem=z_r.at[w, d, s],
            device_id=(lax.rem(r + way, NZ), c), device_id_type=MESH,
        )

    def z_event(w, s):
        for d in range(2):
            if s > 0:
                along_z(w, d, s - 1).wait_recv()
            if s < 4:
                along_z(w, d, s).start()

    def solve(load, put):
        for m in range(4):
            total = None
            for n in range(m + 1):
                part = jnp.dot(
                    linv[256 * m : 256 * m + 256, 256 * n : 256 * n + 256], load(n),
                    preferred_element_type=jnp.float32,
                )
                total = part if total is None else total + part
            put(m, total.astype(jnp.bfloat16))

    def factor_turned():
        for m in range(4):
            for n in range(m + 1):
                linv[256 * m : 256 * m + 256, 256 * n : 256 * n + 256] = lg[
                    n, :, :, :, 256 * m : 256 * m + 256
                ].reshape(256, 256).T

    def columns_solved():
        def tile(t, carry):
            def put(m, block):
                sjt[t, :, 256 * m : 256 * m + 256] = block.T

            solve(lambda n: jg[t, 0, 256 * n : 256 * n + 256, :], put)
            return carry

        lax.fori_loop(0, 2, tile, 0)

    def slots_solved(first):
        def slot(i, carry):
            s = first + i
            cols = pl.ds(pl.multiple_of(s * 256, 256), 256)

            def put(m, block):
                sa[s, 256 * m : 256 * m + 256, :] = block

            solve(lambda n: vg[n, :, :, :, cols].reshape(256, 256), put)
            solved_out[s] = sa[s, pl.ds(pl.multiple_of(c * 32, 32), 32), :]
            return carry

        lax.fori_loop(0, 4, slot, 0)

    def cores():
        def slot(s, carry):
            for t in range(2):

                @pl.when(c + 32 * t <= s * NZ + r)
                def _():
                    core[s, t] = jnp.dot(
                        sjt[t], sa[s], preferred_element_type=jnp.float32
                    ).astype(jnp.bfloat16)

            return carry

        lax.fori_loop(0, 8, slot, 0)

    scatter_event(0)
    near_start(V, 0)
    near_start(V, 1)
    for i in (4, 3, 5, 2, 6, 1, 7):
        when(linv_live(r), lambda: linv_copy(i).start())
    scatter_event(1)
    scattered(0)
    z_event(0, 0)
    for i in range(1, NZ):
        when(linv_live(lax.rem(r + NZ - i, NZ)), lambda: linv_copy(i).wait_recv())
    near_start(L, 0)
    when(near_live(L, 1, 0), lambda: near_start(L, 1))
    far_start(V, 0)
    far_start(V, 1)
    scattered(1)
    z_event(1, 0)
    z_event(0, 1)
    far_start(L, 1)
    far_start(L, 0)
    z_event(1, 1)
    for p in range(2):
        far_more(V, p, 0)
        far_more(V, p, 1)
    z_event(0, 2)
    for p in (1, 0):
        far_more(L, p, 0)
        far_more(L, p, 1)
    z_event(1, 2)
    far_end(V, 0)
    far_end(V, 1)
    z_event(0, 3)
    far_end(L, 1)
    far_end(L, 0)
    z_event(1, 3)
    sib_got(L, 0)
    sib_got(L, 1)
    factor_turned()
    z_event(0, 4)
    columns_solved()
    sib_got(V, 0)
    slots_solved(0)
    z_event(1, 4)
    out_u = pltpu.make_async_copy(jg.at[:, 1], u_out, out_sem.at[1])
    out_u.start()
    sib_got(V, 1)
    slots_solved(4)
    cores()
    out_core = pltpu.make_async_copy(core, core_out, out_sem.at[0])
    out_core.start()

    def all_sent(sem, ref):
        pltpu.make_async_remote_copy(
            src_ref=ref, dst_ref=ref, send_sem=sem, recv_sem=l_r.at[0],
            device_id=(r, sib), device_id_type=MESH,
        ).wait_send()

    for sem, rows in (
        (v_s.at[0], 192), (v_s.at[1], 768), (v_s.at[2], 1024), (v_s.at[3], 720), (z_s, 896),
    ):
        all_sent(sem, linv.at[pl.ds(0, rows)])
    when(
        near_live(L, 1, 0),
        lambda: all_sent(v_s.at[4], linv.at[pl.ds(0, 48)]),
    )
    for i in range(1, NZ):
        when(linv_live(r), lambda: linv_copy(i).wait_send())
    for w in range(2):
        for q in range(4):
            when(not_me(q), lambda: scatter(q, w).wait_send())
    out_core.wait()
    out_u.wait()


def gather(ranks, panel_index, tile_u, tile_v, inverse_factor):
    dma = pltpu.SemaphoreType.DMA
    bf16 = jnp.bfloat16
    vmem = pl.BlockSpec(memory_space=pltpu.VMEM)
    smem = pl.BlockSpec(memory_space=pltpu.SMEM)
    hbm = pl.BlockSpec(memory_space=pl.ANY)
    return pl.pallas_call(
        gather_kernel,
        out_shape=(
            jax.ShapeDtypeStruct((8, 2, 256, 256), bf16),
            jax.ShapeDtypeStruct((2, 1024, 256), bf16),
            jax.ShapeDtypeStruct((8, 32, 256), bf16),
        ),
        in_specs=[smem, smem, hbm, hbm, hbm],
        out_specs=[hbm, hbm, vmem],
        scratch_shapes=[
            pltpu.VMEM((32, 8, 256), bf16),
            pltpu.VMEM((32, 8, 256), bf16),
            pltpu.VMEM((4, 2, 2, 32, 256), bf16),
            pltpu.VMEM((NY, NX, 2, 32, 2 * VW), bf16),
            pltpu.VMEM((NY, NX, 2, 32, 2 * LW), bf16),
            pltpu.VMEM((2, 2, 1024, 256), bf16),
            pltpu.VMEM((1024, 1024), bf16),
            pltpu.VMEM((2, 256, 1024), bf16),
            pltpu.VMEM((8, 1024, 256), bf16),
            pltpu.VMEM((8, 2, 256, 256), bf16),
            dma((2, 4)), dma((2, 4)),
            dma((7,)), dma((7,)),
            dma((2, 2, 3)), dma((2, 2, 4)), dma((2, 2)),
            dma, dma((2, 2, 4)),
            dma((5,)), dma((3,)),
        ],
        compiler_params=pltpu.CompilerParams(
            collective_id=0, has_side_effects=True, vmem_limit_bytes=60 * 2**20
        ),
        name="gather",
    )(ranks, panel_index, tile_u, tile_v, inverse_factor)


def update_kernel(k_ref, core_ref, u_ref, solved_ref, out_ref, solved_out):
    a = pl.program_id(0)

    @pl.when(a == 0)
    def _():
        solved_out[...] = jnp.swapaxes(solved_ref[...], 0, 1)

    row_tile = a * NZ + lax.axis_index("row")
    for t in range(2):
        col_tile = lax.axis_index("col") + 32 * t
        live = jnp.logical_and(col_tile > k_ref[0], col_tile <= row_tile)

        @pl.when(live)
        def _():
            for m in range(4):
                out_ref[0, t, 256 * m : 256 * m + 256, :] = jnp.dot(
                    u_ref[t, 256 * m : 256 * m + 256, :], core_ref[0, t],
                    preferred_element_type=jnp.float32,
                ).astype(jnp.bfloat16)

        @pl.when(jnp.logical_not(live))
        def _():
            out_ref[0, t] = jnp.zeros((1024, 256), jnp.bfloat16)


def update(panel_index, core, column_u, solved):
    return pl.pallas_call(
        update_kernel,
        grid=(8,),
        out_shape=(
            jax.ShapeDtypeStruct((8, 2, 1024, 256), jnp.bfloat16),
            jax.ShapeDtypeStruct((32, 8, 256), jnp.bfloat16),
        ),
        in_specs=[
            pl.BlockSpec(memory_space=pltpu.SMEM),
            pl.BlockSpec((1, 2, 256, 256), lambda a: (a, 0, 0, 0)),
            pl.BlockSpec((2, 1024, 256), lambda a: (0, 0, 0)),
            pl.BlockSpec((8, 32, 256), lambda a: (0, 0, 0)),
        ],
        out_specs=[
            pl.BlockSpec((1, 2, 1024, 256), lambda a: (a, 0, 0, 0)),
            pl.BlockSpec((32, 8, 256), lambda a: (0, 0, 0)),
        ],
        compiler_params=pltpu.CompilerParams(
            dimension_semantics=("arbitrary",), vmem_limit_bytes=60 * 2**20
        ),
        name="update",
    )(panel_index, core, column_u, solved)


def per_device(tile_u, tile_v, inverse_factor, ranks, panel_index):
    core, column_u, solved = gather(ranks, panel_index, tile_u, tile_v, inverse_factor.T)
    return update(panel_index, core, column_u, solved)


def solution(mesh):
    placed = (P("col", "row", None), P("col", "row", None), P("row", "col"), P("row"), P())
    return jax.shard_map(
        per_device,
        mesh=mesh,
        in_specs=placed,
        out_specs=(P("row", "col", None, None), P("col", "row", None)),
        check_vma=False,
    )
```

```python
import jax
import jax.numpy as jnp
from jax import lax
from jax.experimental import pallas as pl
from jax.experimental.pallas import tpu as pltpu
from jax.sharding import PartitionSpec as P

MESH = pl.DeviceIdType.MESH
NZ = 8
NX = 4
NY = 4
VW = 1024
LW = 512


def dev(r, c):
    return (r, c)


def gather_kernel(
    rank_ref, k_ref, u_hbm, v_hbm, lt_hbm, core_out, u_out, solved_out,
    u_ref, v_ref, js, vg, lg, jg, linv, sjt, sa, core,
    sc_s, sc_r, l_s, l_r, near_r, far_r, sib_r, z_s, z_r, v_s, out_sem, core_s,
):
    r = lax.axis_index("row")
    c = lax.axis_index("col")
    y = lax.div(c, 8)
    x = lax.rem(lax.div(c, 2), 4)
    k = lax.rem(c, 2)
    sib = c + 1 - 2 * k
    home = lax.rem(c, 8)
    spread = lax.div(c, 4)
    itself = jnp.logical_and(spread == r, home == r)
    xp = y * 8 + lax.rem(x + 1, 4) * 2 + k
    xm = y * 8 + lax.rem(x + 3, 4) * 2 + k
    yp = lax.rem(y + 1, 4) * 8 + x * 2 + k
    ym = lax.rem(y + 3, 4) * 8 + x * 2 + k
    xx = y * 8 + lax.rem(x + 2, 4) * 2 + k
    yy = lax.rem(y + 2, 4) * 8 + x * 2 + k

    def when(cond, act):
        if cond is True:
            act()
        else:
            pl.when(cond)(act)

    l_at = pl.multiple_of(r * 128, 128)
    loads = (
        pltpu.make_async_copy(v_hbm, v_ref, out_sem.at[0]),
        pltpu.make_async_copy(lt_hbm, lg.at[y, x, k, :, pl.ds(l_at, 128)], out_sem.at[1]),
        pltpu.make_async_copy(u_hbm, u_ref, out_sem.at[2]),
    )
    for load in loads:
        load.start()
    barrier = pltpu.get_barrier_semaphore()

    def hello(rr, cc):
        pl.semaphore_signal(barrier, inc=1, device_id=(rr, cc), device_id_type=MESH)

    for i in range(1, NZ):
        hello(lax.rem(r + i, NZ), c)
    for cc in (xp, xm, xx, yp, ym, yy, sib):
        hello(r, cc)
    for i in range(4):
        cc = 4 * r + i
        when(
            jnp.logical_not(jnp.logical_and(home == r, cc == c)),
            lambda cc=cc: hello(home, cc),
        )

    for load in loads:
        load.wait()
    lane = lax.broadcasted_iota(jnp.int32, (32, 256), 1)
    by_slot = jnp.swapaxes(v_ref[...], 0, 1)
    for s in range(8):
        width = jnp.where(s * NZ + r > k_ref[0], rank_ref[s], 0)
        kept = by_slot[s] * (lane < width).astype(jnp.bfloat16)
        js[s % 4, 0, s // 4] = kept
        vg[y, x, k, :, 256 * s : 256 * s + 256] = kept
    by_slot = jnp.swapaxes(u_ref[...], 0, 1)
    for s in range(8):
        js[s % 4, 1, s // 4] = by_slot[s]

    @pl.when(itself)
    def _():
        pl.semaphore_wait(barrier, 17)

    @pl.when(jnp.logical_not(itself))
    def _():
        pl.semaphore_wait(barrier, 18)

    def scatter(q, w):
        return pltpu.make_async_remote_copy(
            src_ref=js.at[q, w],
            dst_ref=jg.at[:, w, pl.ds(pl.multiple_of(c * 32, 32), 32)],
            send_sem=sc_s.at[w, q],
            recv_sem=sc_r.at[w, lax.rem(c, 4)],
            device_id=(spread, 8 * q + r),
            device_id_type=MESH,
        )

    def not_me(q):
        return jnp.logical_not(jnp.logical_and(spread == r, 8 * q + r == c))

    def scatter_event(w):
        for q in range(4):
            when(not_me(q), lambda: scatter(q, w).start())

            @pl.when(jnp.logical_not(not_me(q)))
            def _():
                jg[:, w, pl.ds(pl.multiple_of(c * 32, 32), 32)] = js[q, w]

    def scattered(w):
        for i in range(4):

            @pl.when(jnp.logical_not(jnp.logical_and(home == r, 4 * r + i == c)))
            def _():
                pltpu.make_async_remote_copy(
                    src_ref=js.at[0, w],
                    dst_ref=jg.at[:, w, pl.ds(pl.multiple_of((4 * r + i) * 32, 32), 32)],
                    send_sem=sc_s.at[w, 0],
                    recv_sem=sc_r.at[w, i],
                    device_id=(home, 4 * r + i),
                    device_id_type=MESH,
                ).wait_recv()

    def linv_copy(i):
        return pltpu.make_async_remote_copy(
            src_ref=lg.at[y, x, k, :, pl.ds(l_at, 128)],
            dst_ref=lg.at[y, x, k, :, pl.ds(l_at, 128)],
            send_sem=l_s.at[i - 1],
            recv_sem=l_r.at[i - 1],
            device_id=(lax.rem(r + i, NZ), c),
            device_id_type=MESH,
        )

    def linv_live(rr):
        return jnp.logical_or(y < 2, rr >= 4)

    V, L = 0, 1
    came = (-1, 1, 2)

    def at(pos, off):
        return lax.rem(pos + 4 + off, 4)

    def columns(kind, p, half=None):
        width = VW if kind == V else LW
        first = width * (p if kind == V else 1 - p)
        if half is not None:
            width //= 2
            first += width * half
        return pl.ds(first, width)

    def near_live(kind, p, off):
        if kind == V or p == 0:
            return True
        return at(y, off) < 2

    def near(kind, p, m, off=0):
        buf = vg if kind == V else lg
        cols = columns(kind, p)
        if p == 0:
            ref = buf.at[y, at(x, off), k, :, cols]
            to = (xp, xm, xx)[m]
        else:
            ref = buf.at[at(y, off), x, k, :, cols]
            to = (yp, ym, yy)[m]
        return pltpu.make_async_remote_copy(
            src_ref=ref, dst_ref=ref,
            send_sem=v_s.at[4 if kind == L and p == 1 else 3 if kind == L else 0],
            recv_sem=near_r.at[kind, p, m],
            device_id=(r, to), device_id_type=MESH,
        )

    def group(kind, p, off, half=None):
        cols = columns(kind, p, half)
        if kind == V:
            if p == 0:
                return vg.at[at(y, off), :, k, :, cols]
            return vg.at[:, at(x, off), k, :, cols]
        if p == 0:
            return lg.at[at(y, off), :, k, :, cols]
        return lg.at[pl.ds(0, 2), at(x, off), k, :, cols]

    def far(kind, p, m):
        if m < 2:
            ref = group(kind, p, 0)
        else:
            ref = group(kind, p, came[m - 2], m - 2)
        if p == 0:
            to = ym if m % 2 else yp
        else:
            to = xm if m % 2 else xp
        return pltpu.make_async_remote_copy(
            src_ref=ref, dst_ref=ref,
            send_sem=v_s.at[1 if kind == V else 3], recv_sem=far_r.at[kind, p, m],
            device_id=(r, to), device_id_type=MESH,
        )

    def sibling(kind, p, off):
        ref = group(kind, p, off)
        return pltpu.make_async_remote_copy(
            src_ref=ref, dst_ref=ref,
            send_sem=v_s.at[2 if kind == V else 3], recv_sem=sib_r.at[kind, p],
            device_id=(r, sib), device_id_type=MESH,
        )

    def near_start(kind, p):
        for m in (2, 0, 1):
            near(kind, p, m).start()

    def far_start(kind, p):
        for m in range(3):
            when(
                near_live(kind, p, came[m]),
                lambda: near(kind, p, m, came[m]).wait_recv(),
            )
        far(kind, p, 0).start()
        far(kind, p, 1).start()
        sibling(kind, p, 0).start()

    def far_more(kind, p, m):
        far(kind, p, m).wait_recv()
        far(kind, p, m + 2).start()
        sibling(kind, p, came[m]).start()

    def far_end(kind, p):
        far(kind, p, 2).wait_recv()
        far(kind, p, 3).wait_recv()
        sibling(kind, p, 2).start()

    def sib_got(kind, p):
        cols = columns(kind, p)
        if kind == V:
            ref = vg.at[:, :, 1 - k, :, cols]
        elif p == 0:
            ref = lg.at[:, :, 1 - k, :, cols]
        else:
            ref = lg.at[pl.ds(0, 2), :, 1 - k, :, cols]
        pltpu.make_async_remote_copy(
            src_ref=ref, dst_ref=ref, send_sem=v_s.at[2], recv_sem=sib_r.at[kind, p],
            device_id=(r, sib), device_id_type=MESH,
        ).wait_recv()

    def along_z(w, d, s):
        way = 1 if d == 0 else NZ - 1
        block = lax.rem(r + s * (NZ - way), NZ)
        rows = pl.ds(pl.multiple_of(block * 128, 128), 128)
        ref = jg.at[:, w, rows] if s < 3 else jg.at[d, w, rows]
        return pltpu.make_async_remote_copy(
            src_ref=ref, dst_ref=ref,
            send_sem=z_s, recv_sem=z_r.at[w, d, s],
            device_id=(lax.rem(r + way, NZ), c), device_id_type=MESH,
        )

    def z_event(w, s):
        for d in range(2):
            if s > 0:
                along_z(w, d, s - 1).wait_recv()
            if s < 4:
                along_z(w, d, s).start()

    def solve(load, put):
        for m in range(4):
            total = None
            for n in range(m + 1):
                part = jnp.dot(
                    linv[256 * m : 256 * m + 256, 256 * n : 256 * n + 256], load(n),
                    preferred_element_type=jnp.float32,
                )
                total = part if total is None else total + part
            put(m, total.astype(jnp.bfloat16))

    def factor_turned():
        for m in range(4):
            for n in range(m + 1):
                linv[256 * m : 256 * m + 256, 256 * n : 256 * n + 256] = lg[
                    n, :, :, :, 256 * m : 256 * m + 256
                ].reshape(256, 256).T

    def columns_solved():
        def tile(t, carry):
            def put(m, block):
                sjt[t, :, 256 * m : 256 * m + 256] = block.T

            solve(lambda n: jg[t, 0, 256 * n : 256 * n + 256, :], put)
            return carry

        lax.fori_loop(0, 2, tile, 0)

    def slots(first):
        def slot(i, carry):
            s = first + i
            cols = pl.ds(pl.multiple_of(s * 256, 256), 256)

            def put(m, block):
                sa[256 * m : 256 * m + 256, :] = block

            solve(lambda n: vg[n, :, :, :, cols].reshape(256, 256), put)
            solved_out[s] = sa[pl.ds(pl.multiple_of(c * 32, 32), 32), :]
            for t in range(2):

                @pl.when(c + 32 * t <= s * NZ + r)
                def _():
                    core[s, t] = jnp.dot(
                        sjt[t], sa[...], preferred_element_type=jnp.float32
                    ).astype(jnp.bfloat16)

            core_copy(s).start()
            return carry

        lax.fori_loop(0, 4, slot, 0)

    def core_copy(s):
        return pltpu.make_async_copy(core.at[s], core_out.at[s], core_s.at[s])

    scatter_event(0)
    near_start(V, 0)
    near_start(V, 1)
    for i in (4, 3, 5, 2, 6, 1, 7):
        when(linv_live(r), lambda: linv_copy(i).start())
    scatter_event(1)
    scattered(0)
    z_event(0, 0)
    for i in range(1, NZ):
        when(linv_live(lax.rem(r + NZ - i, NZ)), lambda: linv_copy(i).wait_recv())
    near_start(L, 0)
    when(near_live(L, 1, 0), lambda: near_start(L, 1))
    far_start(V, 0)
    far_start(V, 1)
    scattered(1)
    z_event(1, 0)
    z_event(0, 1)
    far_start(L, 1)
    far_start(L, 0)
    z_event(1, 1)
    for p in range(2):
        far_more(V, p, 0)
        far_more(V, p, 1)
    z_event(0, 2)
    for p in (1, 0):
        far_more(L, p, 0)
        far_more(L, p, 1)
    z_event(1, 2)
    far_end(V, 0)
    far_end(V, 1)
    z_event(0, 3)
    far_end(L, 1)
    far_end(L, 0)
    z_event(1, 3)
    sib_got(L, 0)
    sib_got(L, 1)
    factor_turned()
    z_event(0, 4)
    columns_solved()
    sib_got(V, 0)
    slots(0)
    z_event(1, 4)
    out_u = pltpu.make_async_copy(jg.at[:, 1], u_out, out_sem.at[1])
    out_u.start()
    sib_got(V, 1)
    slots(4)

    def all_sent(sem, ref):
        pltpu.make_async_remote_copy(
            src_ref=ref, dst_ref=ref, send_sem=sem, recv_sem=l_r.at[0],
            device_id=(r, sib), device_id_type=MESH,
        ).wait_send()

    for sem, rows in (
        (v_s.at[0], 192), (v_s.at[1], 768), (v_s.at[2], 1024), (v_s.at[3], 720), (z_s, 896),
    ):
        all_sent(sem, linv.at[pl.ds(0, rows)])
    when(
        near_live(L, 1, 0),
        lambda: all_sent(v_s.at[4], linv.at[pl.ds(0, 48)]),
    )
    for i in range(1, NZ):
        when(linv_live(r), lambda: linv_copy(i).wait_send())
    for w in range(2):
        for q in range(4):
            when(not_me(q), lambda: scatter(q, w).wait_send())
    for s in range(8):
        core_copy(s).wait()
    out_u.wait()


def gather(ranks, panel_index, tile_u, tile_v, inverse_factor):
    dma = pltpu.SemaphoreType.DMA
    bf16 = jnp.bfloat16
    vmem = pl.BlockSpec(memory_space=pltpu.VMEM)
    smem = pl.BlockSpec(memory_space=pltpu.SMEM)
    hbm = pl.BlockSpec(memory_space=pl.ANY)
    return pl.pallas_call(
        gather_kernel,
        out_shape=(
            jax.ShapeDtypeStruct((8, 2, 256, 256), bf16),
            jax.ShapeDtypeStruct((2, 1024, 256), bf16),
            jax.ShapeDtypeStruct((8, 32, 256), bf16),
        ),
        in_specs=[smem, smem, hbm, hbm, hbm],
        out_specs=[hbm, hbm, vmem],
        scratch_shapes=[
            pltpu.VMEM((32, 8, 256), bf16),
            pltpu.VMEM((32, 8, 256), bf16),
            pltpu.VMEM((4, 2, 2, 32, 256), bf16),
            pltpu.VMEM((NY, NX, 2, 32, 2 * VW), bf16),
            pltpu.VMEM((NY, NX, 2, 32, 2 * LW), bf16),
            pltpu.VMEM((2, 2, 1024, 256), bf16),
            pltpu.VMEM((1024, 1024), bf16),
            pltpu.VMEM((2, 256, 1024), bf16),
            pltpu.VMEM((1024, 256), bf16),
            pltpu.VMEM((8, 2, 256, 256), bf16),
            dma((2, 4)), dma((2, 4)),
            dma((7,)), dma((7,)),
            dma((2, 2, 3)), dma((2, 2, 4)), dma((2, 2)),
            dma, dma((2, 2, 4)),
            dma((5,)), dma((3,)), dma((8,)),
        ],
        compiler_params=pltpu.CompilerParams(
            collective_id=0, has_side_effects=True, vmem_limit_bytes=60 * 2**20
        ),
        name="gather",
    )(ranks, panel_index, tile_u, tile_v, inverse_factor)


def update_kernel(
    k_ref, core_hbm, u_hbm, solved_ref, out_ref, solved_out,
    core_ref, u_ref, zero, block, sem, core_sem, u_sem,
):
    r = lax.axis_index("row")
    c = lax.axis_index("col")

    def is_live(s, t):
        col_tile = c + 32 * t
        return jnp.logical_and(col_tile > k_ref[0], col_tile <= s * NZ + r)

    def send(src, s, t):
        return pltpu.make_async_copy(src, out_ref.at[s, t], sem.at[s, t])

    def core_load(s):
        return pltpu.make_async_copy(core_hbm.at[s], core_ref.at[s], core_sem.at[s])

    u_load = pltpu.make_async_copy(u_hbm, u_ref, u_sem)
    u_load.start()
    for s in range(8):
        core_load(s).start()
    zero[...] = jnp.zeros((1024, 256), jnp.bfloat16)

    def dead(s, carry):
        for t in range(2):

            @pl.when(jnp.logical_not(is_live(s, t)))
            def _():
                send(zero, s, t).start()

        return carry

    def live(s, carry):
        core_load(s).wait()
        for t in range(2):

            @pl.when(is_live(s, t))
            def _():
                for m in range(4):
                    block[s, t, 256 * m : 256 * m + 256, :] = jnp.dot(
                        u_ref[t, 256 * m : 256 * m + 256, :], core_ref[s, t],
                        preferred_element_type=jnp.float32,
                    ).astype(jnp.bfloat16)
                send(block.at[s, t], s, t).start()

        return carry

    def done(s, carry):
        for t in range(2):
            send(block.at[s, t], s, t).wait()
        return carry

    lax.fori_loop(0, 8, dead, 0)
    u_load.wait()
    lax.fori_loop(0, 8, live, 0)
    solved_out[...] = jnp.swapaxes(solved_ref[...], 0, 1)
    lax.fori_loop(0, 8, done, 0)


def update(panel_index, core, column_u, solved):
    vmem = pl.BlockSpec(memory_space=pltpu.VMEM)
    hbm = pl.BlockSpec(memory_space=pl.ANY)
    return pl.pallas_call(
        update_kernel,
        out_shape=(
            jax.ShapeDtypeStruct((8, 2, 1024, 256), jnp.bfloat16),
            jax.ShapeDtypeStruct((32, 8, 256), jnp.bfloat16),
        ),
        in_specs=[pl.BlockSpec(memory_space=pltpu.SMEM), hbm, hbm, vmem],
        out_specs=[hbm, vmem],
        scratch_shapes=[
            pltpu.VMEM((8, 2, 256, 256), jnp.bfloat16),
            pltpu.VMEM((2, 1024, 256), jnp.bfloat16),
            pltpu.VMEM((1024, 256), jnp.bfloat16),
            pltpu.VMEM((8, 2, 1024, 256), jnp.bfloat16),
            pltpu.SemaphoreType.DMA((8, 2)),
            pltpu.SemaphoreType.DMA((8,)),
            pltpu.SemaphoreType.DMA,
        ],
        compiler_params=pltpu.CompilerParams(vmem_limit_bytes=60 * 2**20),
        name="update",
    )(panel_index, core, column_u, solved)


def per_device(tile_u, tile_v, inverse_factor, ranks, panel_index):
    core, column_u, solved = gather(ranks, panel_index, tile_u, tile_v, inverse_factor.T)
    return update(panel_index, core, column_u, solved)


def solution(mesh):
    placed = (P("col", "row", None), P("col", "row", None), P("row", "col"), P("row"), P())
    return jax.shard_map(
        per_device,
        mesh=mesh,
        in_specs=placed,
        out_specs=(P("row", "col", None, None), P("col", "row", None)),
        check_vma=False,
    )
```

```python
import jax
import jax.numpy as jnp
from jax import lax
from jax.experimental import pallas as pl
from jax.experimental.pallas import tpu as pltpu
from jax.sharding import PartitionSpec as P

MESH = pl.DeviceIdType.MESH
NZ = 8
NX = 4
NY = 4
VW = 1024
LW = 512


def dev(r, c):
    return (r, c)


def gather_kernel(
    rank_ref, k_ref, u_hbm, v_hbm, lt_hbm, core_out, u_out, solved_out,
    u_ref, v_ref, js, vg, lg, jg, linv, sjt, sa, core,
    sc_s, sc_r, l_s, l_r, near_r, far_r, sib_r, z_s, z_r, v_s, out_sem, core_s,
):
    r = lax.axis_index("row")
    c = lax.axis_index("col")
    y = lax.div(c, 8)
    x = lax.rem(lax.div(c, 2), 4)
    k = lax.rem(c, 2)
    sib = c + 1 - 2 * k
    home = lax.rem(c, 8)
    spread = lax.div(c, 4)
    itself = jnp.logical_and(spread == r, home == r)
    xp = y * 8 + lax.rem(x + 1, 4) * 2 + k
    xm = y * 8 + lax.rem(x + 3, 4) * 2 + k
    yp = lax.rem(y + 1, 4) * 8 + x * 2 + k
    ym = lax.rem(y + 3, 4) * 8 + x * 2 + k
    xx = y * 8 + lax.rem(x + 2, 4) * 2 + k
    yy = lax.rem(y + 2, 4) * 8 + x * 2 + k

    def when(cond, act):
        if cond is True:
            act()
        else:
            pl.when(cond)(act)

    l_at = pl.multiple_of(r * 128, 128)
    loads = (
        pltpu.make_async_copy(v_hbm, v_ref, out_sem.at[0]),
        pltpu.make_async_copy(lt_hbm, lg.at[y, x, k, :, pl.ds(l_at, 128)], out_sem.at[1]),
        pltpu.make_async_copy(u_hbm, u_ref, out_sem.at[2]),
    )
    for load in loads:
        load.start()
    barrier = pltpu.get_barrier_semaphore()

    def hello(rr, cc):
        pl.semaphore_signal(barrier, inc=1, device_id=(rr, cc), device_id_type=MESH)

    for i in range(1, NZ):
        hello(lax.rem(r + i, NZ), c)
    for cc in (xp, xm, xx, yp, ym, yy, sib):
        hello(r, cc)
    for i in range(4):
        cc = 4 * r + i
        when(
            jnp.logical_not(jnp.logical_and(home == r, cc == c)),
            lambda cc=cc: hello(home, cc),
        )

    for load in loads:
        load.wait()
    lane = lax.broadcasted_iota(jnp.int32, (32, 256), 1)
    by_slot = jnp.swapaxes(v_ref[...], 0, 1)
    for s in range(8):
        width = jnp.where(s * NZ + r > k_ref[0], rank_ref[s], 0)
        kept = by_slot[s] * (lane < width).astype(jnp.bfloat16)
        js[s % 4, 0, s // 4] = kept
        vg[y, x, k, :, 256 * s : 256 * s + 256] = kept
    by_slot = jnp.swapaxes(u_ref[...], 0, 1)
    for s in range(8):
        js[s % 4, 1, s // 4] = by_slot[s]

    @pl.when(itself)
    def _():
        pl.semaphore_wait(barrier, 17)

    @pl.when(jnp.logical_not(itself))
    def _():
        pl.semaphore_wait(barrier, 18)

    def scatter(q, w):
        return pltpu.make_async_remote_copy(
            src_ref=js.at[q, w],
            dst_ref=jg.at[:, w, pl.ds(pl.multiple_of(c * 32, 32), 32)],
            send_sem=sc_s.at[w, q],
            recv_sem=sc_r.at[w, lax.rem(c, 4)],
            device_id=(spread, 8 * q + r),
            device_id_type=MESH,
        )

    def not_me(q):
        return jnp.logical_not(jnp.logical_and(spread == r, 8 * q + r == c))

    def scatter_event(w):
        for q in range(4):
            when(not_me(q), lambda: scatter(q, w).start())

            @pl.when(jnp.logical_not(not_me(q)))
            def _():
                jg[:, w, pl.ds(pl.multiple_of(c * 32, 32), 32)] = js[q, w]

    def scattered(w):
        for i in range(4):

            @pl.when(jnp.logical_not(jnp.logical_and(home == r, 4 * r + i == c)))
            def _():
                pltpu.make_async_remote_copy(
                    src_ref=js.at[0, w],
                    dst_ref=jg.at[:, w, pl.ds(pl.multiple_of((4 * r + i) * 32, 32), 32)],
                    send_sem=sc_s.at[w, 0],
                    recv_sem=sc_r.at[w, i],
                    device_id=(home, 4 * r + i),
                    device_id_type=MESH,
                ).wait_recv()

    def linv_copy(i):
        return pltpu.make_async_remote_copy(
            src_ref=lg.at[y, x, k, :, pl.ds(l_at, 128)],
            dst_ref=lg.at[y, x, k, :, pl.ds(l_at, 128)],
            send_sem=l_s.at[i - 1],
            recv_sem=l_r.at[i - 1],
            device_id=(lax.rem(r + i, NZ), c),
            device_id_type=MESH,
        )

    def linv_live(rr):
        return jnp.logical_or(y < 2, rr >= 4)

    V, L = 0, 1
    came = (-1, 1, 2)

    def at(pos, off):
        return lax.rem(pos + 4 + off, 4)

    def columns(kind, p, half=None, part=None):
        width = VW if kind == V else LW
        first = width * (p if kind == V else 1 - p)
        for cut in (part, half):
            if cut is not None:
                width //= 2
                first += width * cut
        return pl.ds(first, width)

    def near_live(kind, p, off):
        if kind == V or p == 0:
            return True
        return at(y, off) < 2

    def near(kind, p, m, off=0, half=None):
        buf = vg if kind == V else lg
        cols = columns(kind, p, half)
        to = ((xp, xm, xx), (yp, ym, yy))[p][m if kind == L else m % 2]
        if p == 0:
            ref = buf.at[y, at(x, off), k, :, cols]
        else:
            ref = buf.at[at(y, off), x, k, :, cols]
        return pltpu.make_async_remote_copy(
            src_ref=ref, dst_ref=ref,
            send_sem=v_s.at[4 if kind == L and p == 1 else 3 if kind == L else 0],
            recv_sem=near_r.at[kind, p, m],
            device_id=(r, to), device_id_type=MESH,
        )

    def group(kind, p, part, off, half=None):
        cols = columns(kind, p, half, part)
        if kind == V:
            if p == 0:
                return vg.at[at(y, off), :, k, :, cols]
            return vg.at[:, at(x, off), k, :, cols]
        if p == 0:
            return lg.at[at(y, off), :, k, :, cols]
        return lg.at[pl.ds(0, 2), at(x, off), k, :, cols]

    def far(kind, p, part, m):
        if m < 2:
            ref = group(kind, p, part, 0)
        else:
            ref = group(kind, p, part, came[m - 2], m - 2)
        to = ((yp, ym), (xp, xm))[p][m % 2]
        return pltpu.make_async_remote_copy(
            src_ref=ref, dst_ref=ref,
            send_sem=v_s.at[1 if kind == V else 3],
            recv_sem=far_r.at[kind, p, part or 0, m],
            device_id=(r, to), device_id_type=MESH,
        )

    def sibling(kind, p, part, off):
        ref = group(kind, p, part, off)
        return pltpu.make_async_remote_copy(
            src_ref=ref, dst_ref=ref,
            send_sem=v_s.at[2 if kind == V else 3],
            recv_sem=sib_r.at[kind, p, part or 0],
            device_id=(r, sib), device_id_type=MESH,
        )

    def near_start(kind, p):
        for m in (2, 0, 1) if kind == L else (0, 1):
            near(kind, p, m).start()

    def near_more(p):
        for m in range(2):
            near(V, p, m, came[m]).wait_recv()
            near(V, p, m + 2, came[m], m).start()

    def near_end(kind, p):
        if kind == V:
            for m in range(2):
                near(V, p, m + 2, 2, m).wait_recv()
        else:
            for m in range(3):
                when(
                    near_live(kind, p, came[m]),
                    lambda: near(kind, p, m, came[m]).wait_recv(),
                )

    def far_start(kind, p, part=None):
        far(kind, p, part, 0).start()
        far(kind, p, part, 1).start()
        sibling(kind, p, part, 0).start()

    def far_more(kind, p, part=None):
        for m in range(2):
            far(kind, p, part, m).wait_recv()
            far(kind, p, part, m + 2).start()
            sibling(kind, p, part, came[m]).start()

    def far_end(kind, p, part=None):
        far(kind, p, part, 2).wait_recv()
        far(kind, p, part, 3).wait_recv()
        sibling(kind, p, part, 2).start()

    def sib_got(kind, p, part=None):
        cols = columns(kind, p, None, part)
        if kind == V:
            ref = vg.at[:, :, 1 - k, :, cols]
        elif p == 0:
            ref = lg.at[:, :, 1 - k, :, cols]
        else:
            ref = lg.at[pl.ds(0, 2), :, 1 - k, :, cols]
        pltpu.make_async_remote_copy(
            src_ref=ref, dst_ref=ref, send_sem=v_s.at[2],
            recv_sem=sib_r.at[kind, p, part or 0],
            device_id=(r, sib), device_id_type=MESH,
        ).wait_recv()

    def along_z(w, d, s):
        way = 1 if d == 0 else NZ - 1
        block = lax.rem(r + s * (NZ - way), NZ)
        rows = pl.ds(pl.multiple_of(block * 128, 128), 128)
        ref = jg.at[:, w, rows] if s < 3 else jg.at[d, w, rows]
        return pltpu.make_async_remote_copy(
            src_ref=ref, dst_ref=ref,
            send_sem=z_s, recv_sem=z_r.at[w, d, s],
            device_id=(lax.rem(r + way, NZ), c), device_id_type=MESH,
        )

    def z_event(w, s):
        for d in range(2):
            if s > 0:
                along_z(w, d, s - 1).wait_recv()
            if s < 4:
                along_z(w, d, s).start()

    def solve(load, put):
        for m in range(4):
            total = None
            for n in range(m + 1):
                part = jnp.dot(
                    linv[256 * m : 256 * m + 256, 256 * n : 256 * n + 256], load(n),
                    preferred_element_type=jnp.float32,
                )
                total = part if total is None else total + part
            put(m, total.astype(jnp.bfloat16))

    def factor_turned():
        for m in range(4):
            for n in range(m + 1):
                linv[256 * m : 256 * m + 256, 256 * n : 256 * n + 256] = lg[
                    n, :, :, :, 256 * m : 256 * m + 256
                ].reshape(256, 256).T

    def columns_solved():
        def tile(t, carry):
            def put(m, block):
                sjt[t, :, 256 * m : 256 * m + 256] = block.T

            solve(lambda n: jg[t, 0, 256 * n : 256 * n + 256, :], put)
            return carry

        lax.fori_loop(0, 2, tile, 0)

    def slots(first):
        def slot(i, carry):
            s = first + i
            cols = pl.ds(pl.multiple_of(s * 256, 256), 256)

            def put(m, block):
                sa[256 * m : 256 * m + 256, :] = block

            solve(lambda n: vg[n, :, :, :, cols].reshape(256, 256), put)
            solved_out[s] = sa[pl.ds(pl.multiple_of(c * 32, 32), 32), :]
            for t in range(2):

                @pl.when(c + 32 * t <= s * NZ + r)
                def _():
                    core[s, t] = jnp.dot(
                        sjt[t], sa[...], preferred_element_type=jnp.float32
                    ).astype(jnp.bfloat16)

            core_copy(s).start()
            return carry

        lax.fori_loop(0, 2, slot, 0)

    def core_copy(s):
        return pltpu.make_async_copy(core.at[s], core_out.at[s], core_s.at[s])

    for i in (4, 3, 5, 2, 6, 1, 7):
        when(linv_live(r), lambda: linv_copy(i).start())
    scatter_event(0)
    near_start(V, 0)
    near_start(V, 1)
    scatter_event(1)
    for i in range(1, NZ):
        when(linv_live(lax.rem(r + NZ - i, NZ)), lambda: linv_copy(i).wait_recv())
    near_start(L, 0)
    when(near_live(L, 1, 0), lambda: near_start(L, 1))
    scattered(0)
    z_event(0, 0)
    near_more(0)
    near_more(1)
    scattered(1)
    z_event(1, 0)
    for p in (1, 0):
        near_end(L, p)
        far_start(L, p)
    z_event(0, 1)
    for p in (1, 0):
        near_end(V, p)
        far_start(V, p, 0)
    z_event(1, 1)
    far_more(L, 1)
    far_start(V, 1, 1)
    z_event(0, 2)
    far_more(L, 0)
    far_start(V, 0, 1)
    far_more(V, 1, 0)
    far_end(L, 1)
    z_event(1, 2)
    far_more(V, 0, 0)
    far_more(V, 1, 1)
    far_end(L, 0)
    z_event(0, 3)
    far_end(V, 1, 0)
    z_event(1, 3)
    far_more(V, 0, 1)
    sib_got(L, 1)
    sib_got(L, 0)
    factor_turned()
    z_event(0, 4)
    far_end(V, 1, 1)
    far_end(V, 0, 0)
    columns_solved()
    sib_got(V, 1, 0)
    slots(4)
    far_end(V, 0, 1)
    z_event(1, 4)
    out_u = pltpu.make_async_copy(jg.at[:, 1], u_out, out_sem.at[1])
    out_u.start()
    sib_got(V, 0, 0)
    slots(0)
    sib_got(V, 1, 1)
    slots(6)
    sib_got(V, 0, 1)
    slots(2)

    def all_sent(sem, ref):
        pltpu.make_async_remote_copy(
            src_ref=ref, dst_ref=ref, send_sem=sem, recv_sem=l_r.at[0],
            device_id=(r, sib), device_id_type=MESH,
        ).wait_send()

    for sem, rows in (
        (v_s.at[0], 192), (v_s.at[1], 768), (v_s.at[2], 1024), (v_s.at[3], 720), (z_s, 896),
    ):
        all_sent(sem, linv.at[pl.ds(0, rows)])
    when(
        near_live(L, 1, 0),
        lambda: all_sent(v_s.at[4], linv.at[pl.ds(0, 48)]),
    )
    for i in range(1, NZ):
        when(linv_live(r), lambda: linv_copy(i).wait_send())
    for w in range(2):
        for q in range(4):
            when(not_me(q), lambda: scatter(q, w).wait_send())
    for s in range(8):
        core_copy(s).wait()
    out_u.wait()


def gather(ranks, panel_index, tile_u, tile_v, inverse_factor):
    dma = pltpu.SemaphoreType.DMA
    bf16 = jnp.bfloat16
    vmem = pl.BlockSpec(memory_space=pltpu.VMEM)
    smem = pl.BlockSpec(memory_space=pltpu.SMEM)
    hbm = pl.BlockSpec(memory_space=pl.ANY)
    return pl.pallas_call(
        gather_kernel,
        out_shape=(
            jax.ShapeDtypeStruct((8, 2, 256, 256), bf16),
            jax.ShapeDtypeStruct((2, 1024, 256), bf16),
            jax.ShapeDtypeStruct((8, 32, 256), bf16),
        ),
        in_specs=[smem, smem, hbm, hbm, hbm],
        out_specs=[hbm, hbm, vmem],
        scratch_shapes=[
            pltpu.VMEM((32, 8, 256), bf16),
            pltpu.VMEM((32, 8, 256), bf16),
            pltpu.VMEM((4, 2, 2, 32, 256), bf16),
            pltpu.VMEM((NY, NX, 2, 32, 2 * VW), bf16),
            pltpu.VMEM((NY, NX, 2, 32, 2 * LW), bf16),
            pltpu.VMEM((2, 2, 1024, 256), bf16),
            pltpu.VMEM((1024, 1024), bf16),
            pltpu.VMEM((2, 256, 1024), bf16),
            pltpu.VMEM((1024, 256), bf16),
            pltpu.VMEM((8, 2, 256, 256), bf16),
            dma((2, 4)), dma((2, 4)),
            dma((7,)), dma((7,)),
            dma((2, 2, 4)), dma((2, 2, 2, 4)), dma((2, 2, 2)),
            dma, dma((2, 2, 4)),
            dma((5,)), dma((3,)), dma((8,)),
        ],
        compiler_params=pltpu.CompilerParams(
            collective_id=0, has_side_effects=True, vmem_limit_bytes=60 * 2**20
        ),
        name="gather",
    )(ranks, panel_index, tile_u, tile_v, inverse_factor)


def update_kernel(
    k_ref, core_hbm, u_hbm, solved_ref, out_ref, solved_out,
    core_ref, u_ref, zero, block, sem, core_sem, u_sem,
):
    r = lax.axis_index("row")
    c = lax.axis_index("col")

    def is_live(s, t):
        col_tile = c + 32 * t
        return jnp.logical_and(col_tile > k_ref[0], col_tile <= s * NZ + r)

    def send(src, s, t):
        return pltpu.make_async_copy(src, out_ref.at[s, t], sem.at[s, t])

    def core_load(s):
        return pltpu.make_async_copy(core_hbm.at[s], core_ref.at[s], core_sem.at[s])

    u_load = pltpu.make_async_copy(u_hbm, u_ref, u_sem)
    u_load.start()
    for s in range(8):
        core_load(s).start()
    zero[...] = jnp.zeros((1024, 256), jnp.bfloat16)

    def dead(s, carry):
        for t in range(2):

            @pl.when(jnp.logical_not(is_live(s, t)))
            def _():
                send(zero, s, t).start()

        return carry

    def live(s, carry):
        core_load(s).wait()
        for t in range(2):

            @pl.when(is_live(s, t))
            def _():
                for m in range(4):
                    block[s, t, 256 * m : 256 * m + 256, :] = jnp.dot(
                        u_ref[t, 256 * m : 256 * m + 256, :], core_ref[s, t],
                        preferred_element_type=jnp.float32,
                    ).astype(jnp.bfloat16)
                send(block.at[s, t], s, t).start()

        return carry

    def done(s, carry):
        for t in range(2):
            send(block.at[s, t], s, t).wait()
        return carry

    lax.fori_loop(0, 8, dead, 0)
    u_load.wait()
    lax.fori_loop(0, 8, live, 0)
    solved_out[...] = jnp.swapaxes(solved_ref[...], 0, 1)
    lax.fori_loop(0, 8, done, 0)


def update(panel_index, core, column_u, solved):
    vmem = pl.BlockSpec(memory_space=pltpu.VMEM)
    hbm = pl.BlockSpec(memory_space=pl.ANY)
    return pl.pallas_call(
        update_kernel,
        out_shape=(
            jax.ShapeDtypeStruct((8, 2, 1024, 256), jnp.bfloat16),
            jax.ShapeDtypeStruct((32, 8, 256), jnp.bfloat16),
        ),
        in_specs=[pl.BlockSpec(memory_space=pltpu.SMEM), hbm, hbm, vmem],
        out_specs=[hbm, vmem],
        scratch_shapes=[
            pltpu.VMEM((8, 2, 256, 256), jnp.bfloat16),
            pltpu.VMEM((2, 1024, 256), jnp.bfloat16),
            pltpu.VMEM((1024, 256), jnp.bfloat16),
            pltpu.VMEM((8, 2, 1024, 256), jnp.bfloat16),
            pltpu.SemaphoreType.DMA((8, 2)),
            pltpu.SemaphoreType.DMA((8,)),
            pltpu.SemaphoreType.DMA,
        ],
        compiler_params=pltpu.CompilerParams(vmem_limit_bytes=60 * 2**20),
        name="update",
    )(panel_index, core, column_u, solved)


def per_device(tile_u, tile_v, inverse_factor, ranks, panel_index):
    core, column_u, solved = gather(ranks, panel_index, tile_u, tile_v, inverse_factor.T)
    return update(panel_index, core, column_u, solved)


def solution(mesh):
    placed = (P("col", "row", None), P("col", "row", None), P("row", "col"), P("row"), P())
    return jax.shard_map(
        per_device,
        mesh=mesh,
        in_specs=placed,
        out_specs=(P("row", "col", None, None), P("col", "row", None)),
        check_vma=False,
    )
```

```python
import jax
import jax.numpy as jnp
from jax import lax
from jax.experimental import pallas as pl
from jax.experimental.pallas import tpu as pltpu
from jax.sharding import PartitionSpec as P

MESH = pl.DeviceIdType.MESH
NZ = 8
NX = 4
NY = 4
VW = 1024
LW = 512


def dev(r, c):
    return (r, c)


def gather_kernel(
    rank_ref, k_ref, u_hbm, v_hbm, lt_hbm, core_out, u_out, solved_out,
    u_ref, v_ref, js, vg, lg, jg, linv, sjt, sa, core,
    sc_s, sc_r, l_s, l_r, near_r, far_r, sib_r, z_s, z_r, v_s, out_sem, core_s,
):
    r = lax.axis_index("row")
    c = lax.axis_index("col")
    y = lax.div(c, 8)
    x = lax.rem(lax.div(c, 2), 4)
    k = lax.rem(c, 2)
    sib = c + 1 - 2 * k
    home = lax.rem(c, 8)
    spread = lax.div(c, 4)
    itself = jnp.logical_and(spread == r, home == r)
    xp = y * 8 + lax.rem(x + 1, 4) * 2 + k
    xm = y * 8 + lax.rem(x + 3, 4) * 2 + k
    yp = lax.rem(y + 1, 4) * 8 + x * 2 + k
    ym = lax.rem(y + 3, 4) * 8 + x * 2 + k
    xx = y * 8 + lax.rem(x + 2, 4) * 2 + k
    yy = lax.rem(y + 2, 4) * 8 + x * 2 + k

    def when(cond, act):
        if cond is True:
            act()
        else:
            pl.when(cond)(act)

    l_at = pl.multiple_of(r * 128, 128)
    loads = (
        pltpu.make_async_copy(v_hbm, v_ref, out_sem.at[0]),
        pltpu.make_async_copy(lt_hbm, lg.at[y, x, k, :, pl.ds(l_at, 128)], out_sem.at[1]),
        pltpu.make_async_copy(u_hbm, u_ref, out_sem.at[2]),
    )
    for load in loads:
        load.start()
    barrier = pltpu.get_barrier_semaphore()

    def hello(rr, cc):
        pl.semaphore_signal(barrier, inc=1, device_id=(rr, cc), device_id_type=MESH)

    for i in range(1, NZ):
        hello(lax.rem(r + i, NZ), c)
    for cc in (xp, xm, xx, yp, ym, yy, sib):
        hello(r, cc)
    for i in range(4):
        cc = 4 * r + i
        when(
            jnp.logical_not(jnp.logical_and(home == r, cc == c)),
            lambda cc=cc: hello(home, cc),
        )

    for load in loads:
        load.wait()
    lane = lax.broadcasted_iota(jnp.int32, (32, 256), 1)
    by_slot = jnp.swapaxes(v_ref[...], 0, 1)
    for s in range(8):
        width = jnp.where(s * NZ + r > k_ref[0], rank_ref[s], 0)
        kept = by_slot[s] * (lane < width).astype(jnp.bfloat16)
        js[s % 4, 0, s // 4] = kept
        vg[y, x, k, :, 256 * s : 256 * s + 256] = kept
    by_slot = jnp.swapaxes(u_ref[...], 0, 1)
    for s in range(8):
        js[s % 4, 1, s // 4] = by_slot[s]

    @pl.when(itself)
    def _():
        pl.semaphore_wait(barrier, 17)

    @pl.when(jnp.logical_not(itself))
    def _():
        pl.semaphore_wait(barrier, 18)

    def scatter(q, w):
        return pltpu.make_async_remote_copy(
            src_ref=js.at[q, w],
            dst_ref=jg.at[:, w, pl.ds(pl.multiple_of(c * 32, 32), 32)],
            send_sem=sc_s.at[w, q],
            recv_sem=sc_r.at[w, lax.rem(c, 4)],
            device_id=(spread, 8 * q + r),
            device_id_type=MESH,
        )

    def not_me(q):
        return jnp.logical_not(jnp.logical_and(spread == r, 8 * q + r == c))

    def scatter_event(w):
        for q in range(4):
            when(not_me(q), lambda: scatter(q, w).start())

            @pl.when(jnp.logical_not(not_me(q)))
            def _():
                jg[:, w, pl.ds(pl.multiple_of(c * 32, 32), 32)] = js[q, w]

    def scattered(w):
        for i in range(4):

            @pl.when(jnp.logical_not(jnp.logical_and(home == r, 4 * r + i == c)))
            def _():
                pltpu.make_async_remote_copy(
                    src_ref=js.at[0, w],
                    dst_ref=jg.at[:, w, pl.ds(pl.multiple_of((4 * r + i) * 32, 32), 32)],
                    send_sem=sc_s.at[w, 0],
                    recv_sem=sc_r.at[w, i],
                    device_id=(home, 4 * r + i),
                    device_id_type=MESH,
                ).wait_recv()

    def linv_copy(i):
        return pltpu.make_async_remote_copy(
            src_ref=lg.at[y, x, k, :, pl.ds(l_at, 128)],
            dst_ref=lg.at[y, x, k, :, pl.ds(l_at, 128)],
            send_sem=l_s.at[i - 1],
            recv_sem=l_r.at[i - 1],
            device_id=(lax.rem(r + i, NZ), c),
            device_id_type=MESH,
        )

    def linv_live(rr):
        return jnp.logical_or(y < 2, rr >= 4)

    V, L = 0, 1
    came = (-1, 1, 2)

    def at(pos, off):
        return lax.rem(pos + 4 + off, 4)

    def columns(kind, p, half=None, part=None):
        width = VW if kind == V else LW
        first = width * (p if kind == V else 1 - p)
        for cut in (part, half):
            if cut is not None:
                width //= 2
                first += width * cut
        return pl.ds(first, width)

    def near_live(kind, p, off):
        if kind == V or p == 0:
            return True
        return at(y, off) < 2

    def near(kind, p, m, off=0, half=None):
        buf = vg if kind == V else lg
        cols = columns(kind, p, half)
        to = ((xp, xm, xx), (yp, ym, yy))[p][m if kind == L else m % 2]
        if p == 0:
            ref = buf.at[y, at(x, off), k, :, cols]
        else:
            ref = buf.at[at(y, off), x, k, :, cols]
        return pltpu.make_async_remote_copy(
            src_ref=ref, dst_ref=ref,
            send_sem=v_s.at[4 if kind == L and p == 1 else 3 if kind == L else 0],
            recv_sem=near_r.at[kind, p, m],
            device_id=(r, to), device_id_type=MESH,
        )

    def group(kind, p, part, off, half=None):
        cols = columns(kind, p, half, part)
        if kind == V:
            if p == 0:
                return vg.at[at(y, off), :, k, :, cols]
            return vg.at[:, at(x, off), k, :, cols]
        if p == 0:
            return lg.at[at(y, off), :, k, :, cols]
        return lg.at[pl.ds(0, 2), at(x, off), k, :, cols]

    def far(kind, p, part, m):
        if m < 2:
            ref = group(kind, p, part, 0)
        else:
            ref = group(kind, p, part, came[m - 2], m - 2)
        to = ((yp, ym), (xp, xm))[p][m % 2]
        return pltpu.make_async_remote_copy(
            src_ref=ref, dst_ref=ref,
            send_sem=v_s.at[1 if kind == V else 3],
            recv_sem=far_r.at[kind, p, part or 0, m],
            device_id=(r, to), device_id_type=MESH,
        )

    def sibling(kind, p, part, off):
        ref = group(kind, p, part, off)
        return pltpu.make_async_remote_copy(
            src_ref=ref, dst_ref=ref,
            send_sem=v_s.at[2 if kind == V else 3],
            recv_sem=sib_r.at[kind, p, part or 0],
            device_id=(r, sib), device_id_type=MESH,
        )

    def near_start(kind, p):
        for m in (2, 0, 1) if kind == L else (0, 1):
            near(kind, p, m).start()

    def near_more(p):
        for m in range(2):
            near(V, p, m, came[m]).wait_recv()
            near(V, p, m + 2, came[m], m).start()

    def near_end(kind, p):
        if kind == V:
            for m in range(2):
                near(V, p, m + 2, 2, m).wait_recv()
        else:
            for m in range(3):
                when(
                    near_live(kind, p, came[m]),
                    lambda: near(kind, p, m, came[m]).wait_recv(),
                )

    def far_start(kind, p, part=None):
        far(kind, p, part, 0).start()
        far(kind, p, part, 1).start()
        sibling(kind, p, part, 0).start()

    def far_more(kind, p, part=None):
        for m in range(2):
            far(kind, p, part, m).wait_recv()
            far(kind, p, part, m + 2).start()
            sibling(kind, p, part, came[m]).start()

    def far_end(kind, p, part=None):
        far(kind, p, part, 2).wait_recv()
        far(kind, p, part, 3).wait_recv()
        sibling(kind, p, part, 2).start()

    def sib_got(kind, p, part=None):
        cols = columns(kind, p, None, part)
        if kind == V:
            ref = vg.at[:, :, 1 - k, :, cols]
        elif p == 0:
            ref = lg.at[:, :, 1 - k, :, cols]
        else:
            ref = lg.at[pl.ds(0, 2), :, 1 - k, :, cols]
        pltpu.make_async_remote_copy(
            src_ref=ref, dst_ref=ref, send_sem=v_s.at[2],
            recv_sem=sib_r.at[kind, p, part or 0],
            device_id=(r, sib), device_id_type=MESH,
        ).wait_recv()

    def along_z(w, d, s):
        way = 1 if d == 0 else NZ - 1
        block = lax.rem(r + s * (NZ - way), NZ)
        rows = pl.ds(pl.multiple_of(block * 128, 128), 128)
        ref = jg.at[:, w, rows] if s < 3 else jg.at[d, w, rows]
        return pltpu.make_async_remote_copy(
            src_ref=ref, dst_ref=ref,
            send_sem=z_s, recv_sem=z_r.at[w, d, s],
            device_id=(lax.rem(r + way, NZ), c), device_id_type=MESH,
        )

    def z_event(w, s):
        for d in range(2):
            if s > 0:
                along_z(w, d, s - 1).wait_recv()
            if s < 4:
                along_z(w, d, s).start()

    def solve(load, put):
        for m in range(4):
            total = None
            for n in range(m + 1):
                part = jnp.dot(
                    linv[256 * m : 256 * m + 256, 256 * n : 256 * n + 256], load(n),
                    preferred_element_type=jnp.float32,
                )
                total = part if total is None else total + part
            put(m, total.astype(jnp.bfloat16))

    def factor_turned():
        for m in range(4):
            for n in range(m + 1):
                linv[256 * m : 256 * m + 256, 256 * n : 256 * n + 256] = lg[
                    n, :, :, :, 256 * m : 256 * m + 256
                ].reshape(256, 256).T

    def columns_solved():
        def tile(t, carry):
            def put(m, block):
                sjt[t, :, 256 * m : 256 * m + 256] = block.T

            solve(lambda n: jg[t, 0, 256 * n : 256 * n + 256, :], put)
            return carry

        lax.fori_loop(0, 2, tile, 0)

    def slots(first):
        def slot(i, carry):
            s = first + i
            cols = pl.ds(pl.multiple_of(s * 256, 256), 256)

            def put(m, block):
                sa[s, 256 * m : 256 * m + 256, :] = block

            solve(lambda n: vg[n, :, :, :, cols].reshape(256, 256), put)
            solved_out[s] = sa[s, pl.ds(pl.multiple_of(c * 32, 32), 32), :]
            return carry

        lax.fori_loop(0, 2, slot, 0)

    def cores(first):
        def slot(i, carry):
            s = first + i
            for t in range(2):

                @pl.when(c + 32 * t <= s * NZ + r)
                def _():
                    core[s, t] = jnp.dot(
                        sjt[t], sa[s], preferred_element_type=jnp.float32
                    ).astype(jnp.bfloat16)

            core_copy(s).start()
            return carry

        lax.fori_loop(0, 4, slot, 0)

    def core_copy(s):
        return pltpu.make_async_copy(core.at[s], core_out.at[s], core_s.at[s])

    for i in (4, 3, 5, 2, 6, 1, 7):
        when(linv_live(r), lambda: linv_copy(i).start())
    scatter_event(0)
    near_start(V, 0)
    near_start(V, 1)
    scatter_event(1)
    for i in range(1, NZ):
        when(linv_live(lax.rem(r + NZ - i, NZ)), lambda: linv_copy(i).wait_recv())
    near_start(L, 0)
    when(near_live(L, 1, 0), lambda: near_start(L, 1))
    scattered(0)
    z_event(0, 0)
    near_more(0)
    near_more(1)
    scattered(1)
    z_event(1, 0)
    for p in (1, 0):
        near_end(L, p)
        far_start(L, p)
    z_event(0, 1)
    for p in (1, 0):
        near_end(V, p)
        far_start(V, p, 0)
    z_event(1, 1)
    far_more(L, 1)
    far_start(V, 1, 1)
    z_event(0, 2)
    far_more(L, 0)
    far_start(V, 0, 1)
    far_more(V, 1, 0)
    far_end(L, 1)
    z_event(1, 2)
    far_more(V, 0, 0)
    far_more(V, 1, 1)
    far_end(L, 0)
    far_end(V, 1, 0)
    far_more(V, 0, 1)
    sib_got(L, 1)
    sib_got(L, 0)
    factor_turned()
    z_event(0, 3)
    far_end(V, 1, 1)
    far_end(V, 0, 0)
    sib_got(V, 1, 0)
    slots(4)
    far_end(V, 0, 1)
    sib_got(V, 0, 0)
    slots(0)
    z_event(1, 3)
    sib_got(V, 1, 1)
    slots(6)
    sib_got(V, 0, 1)
    slots(2)
    z_event(0, 4)
    columns_solved()
    cores(0)
    z_event(1, 4)
    out_u = pltpu.make_async_copy(jg.at[:, 1], u_out, out_sem.at[1])
    out_u.start()
    cores(4)

    def all_sent(sem, ref):
        pltpu.make_async_remote_copy(
            src_ref=ref, dst_ref=ref, send_sem=sem, recv_sem=l_r.at[0],
            device_id=(r, sib), device_id_type=MESH,
        ).wait_send()

    for sem, rows in (
        (v_s.at[0], 192), (v_s.at[1], 768), (v_s.at[2], 1024), (v_s.at[3], 720), (z_s, 896),
    ):
        all_sent(sem, linv.at[pl.ds(0, rows)])
    when(
        near_live(L, 1, 0),
        lambda: all_sent(v_s.at[4], linv.at[pl.ds(0, 48)]),
    )
    for i in range(1, NZ):
        when(linv_live(r), lambda: linv_copy(i).wait_send())
    for w in range(2):
        for q in range(4):
            when(not_me(q), lambda: scatter(q, w).wait_send())
    for s in range(8):
        core_copy(s).wait()
    out_u.wait()


def gather(ranks, panel_index, tile_u, tile_v, inverse_factor):
    dma = pltpu.SemaphoreType.DMA
    bf16 = jnp.bfloat16
    vmem = pl.BlockSpec(memory_space=pltpu.VMEM)
    smem = pl.BlockSpec(memory_space=pltpu.SMEM)
    hbm = pl.BlockSpec(memory_space=pl.ANY)
    return pl.pallas_call(
        gather_kernel,
        out_shape=(
            jax.ShapeDtypeStruct((8, 2, 256, 256), bf16),
            jax.ShapeDtypeStruct((2, 1024, 256), bf16),
            jax.ShapeDtypeStruct((8, 32, 256), bf16),
        ),
        in_specs=[smem, smem, hbm, hbm, hbm],
        out_specs=[hbm, hbm, vmem],
        scratch_shapes=[
            pltpu.VMEM((32, 8, 256), bf16),
            pltpu.VMEM((32, 8, 256), bf16),
            pltpu.VMEM((4, 2, 2, 32, 256), bf16),
            pltpu.VMEM((NY, NX, 2, 32, 2 * VW), bf16),
            pltpu.VMEM((NY, NX, 2, 32, 2 * LW), bf16),
            pltpu.VMEM((2, 2, 1024, 256), bf16),
            pltpu.VMEM((1024, 1024), bf16),
            pltpu.VMEM((2, 256, 1024), bf16),
            pltpu.VMEM((8, 1024, 256), bf16),
            pltpu.VMEM((8, 2, 256, 256), bf16),
            dma((2, 4)), dma((2, 4)),
            dma((7,)), dma((7,)),
            dma((2, 2, 4)), dma((2, 2, 2, 4)), dma((2, 2, 2)),
            dma, dma((2, 2, 4)),
            dma((5,)), dma((3,)), dma((8,)),
        ],
        compiler_params=pltpu.CompilerParams(
            collective_id=0, has_side_effects=True, vmem_limit_bytes=60 * 2**20
        ),
        name="gather",
    )(ranks, panel_index, tile_u, tile_v, inverse_factor)


def update_kernel(
    k_ref, core_hbm, u_hbm, solved_ref, out_ref, solved_out,
    core_ref, u_ref, zero, block, sem, core_sem, u_sem,
):
    r = lax.axis_index("row")
    c = lax.axis_index("col")

    def is_live(s, t):
        col_tile = c + 32 * t
        return jnp.logical_and(col_tile > k_ref[0], col_tile <= s * NZ + r)

    def send(src, s, t):
        return pltpu.make_async_copy(src, out_ref.at[s, t], sem.at[s, t])

    def core_load(s):
        return pltpu.make_async_copy(core_hbm.at[s], core_ref.at[s], core_sem.at[s])

    u_load = pltpu.make_async_copy(u_hbm, u_ref, u_sem)
    u_load.start()
    for s in range(8):
        core_load(s).start()
    zero[...] = jnp.zeros((1024, 256), jnp.bfloat16)

    def dead(s, carry):
        for t in range(2):

            @pl.when(jnp.logical_not(is_live(s, t)))
            def _():
                send(zero, s, t).start()

        return carry

    def live(s, carry):
        core_load(s).wait()
        for t in range(2):

            @pl.when(is_live(s, t))
            def _():
                block[s, t] = jnp.dot(
                    u_ref[t], core_ref[s, t], preferred_element_type=jnp.float32
                ).astype(jnp.bfloat16)
                send(block.at[s, t], s, t).start()

        return carry

    def done(s, carry):
        for t in range(2):
            send(block.at[s, t], s, t).wait()
        return carry

    lax.fori_loop(0, 8, dead, 0)
    u_load.wait()
    lax.fori_loop(0, 8, live, 0)
    solved_out[...] = jnp.swapaxes(solved_ref[...], 0, 1)
    lax.fori_loop(0, 8, done, 0)


def update(panel_index, core, column_u, solved):
    vmem = pl.BlockSpec(memory_space=pltpu.VMEM)
    hbm = pl.BlockSpec(memory_space=pl.ANY)
    return pl.pallas_call(
        update_kernel,
        out_shape=(
            jax.ShapeDtypeStruct((8, 2, 1024, 256), jnp.bfloat16),
            jax.ShapeDtypeStruct((32, 8, 256), jnp.bfloat16),
        ),
        in_specs=[pl.BlockSpec(memory_space=pltpu.SMEM), hbm, hbm, vmem],
        out_specs=[hbm, vmem],
        scratch_shapes=[
            pltpu.VMEM((8, 2, 256, 256), jnp.bfloat16),
            pltpu.VMEM((2, 1024, 256), jnp.bfloat16),
            pltpu.VMEM((1024, 256), jnp.bfloat16),
            pltpu.VMEM((8, 2, 1024, 256), jnp.bfloat16),
            pltpu.SemaphoreType.DMA((8, 2)),
            pltpu.SemaphoreType.DMA((8,)),
            pltpu.SemaphoreType.DMA,
        ],
        compiler_params=pltpu.CompilerParams(vmem_limit_bytes=60 * 2**20),
        name="update",
    )(panel_index, core, column_u, solved)


def per_device(tile_u, tile_v, inverse_factor, ranks, panel_index):
    core, column_u, solved = gather(ranks, panel_index, tile_u, tile_v, inverse_factor.T)
    return update(panel_index, core, column_u, solved)


def solution(mesh):
    placed = (P("col", "row", None), P("col", "row", None), P("row", "col"), P("row"), P())
    return jax.shard_map(
        per_device,
        mesh=mesh,
        in_specs=placed,
        out_specs=(P("row", "col", None, None), P("col", "row", None)),
        check_vma=False,
    )
```

```python
import jax
import jax.numpy as jnp
from jax import lax
from jax.experimental import pallas as pl
from jax.experimental.pallas import tpu as pltpu
from jax.sharding import PartitionSpec as P

MESH = pl.DeviceIdType.MESH
NZ = 8
NX = 4
NY = 4
VW = 1024
LW = 512


def dev(r, c):
    return (r, c)


def gather_kernel(
    rank_ref, k_ref, u_hbm, v_hbm, lt_hbm, core_out, u_out, solved_out,
    u_ref, v_ref, js, vg, lg, jg, linv, sjt, sa, core,
    sc_s, sc_r, l_s, l_r, near_r, far_r, sib_r, z_s, z_r, v_s, out_sem, core_s,
):
    r = lax.axis_index("row")
    c = lax.axis_index("col")
    y = lax.div(c, 8)
    x = lax.rem(lax.div(c, 2), 4)
    k = lax.rem(c, 2)
    sib = c + 1 - 2 * k
    home = lax.rem(c, 8)
    spread = lax.div(c, 4)
    itself = jnp.logical_and(spread == r, home == r)
    xp = y * 8 + lax.rem(x + 1, 4) * 2 + k
    xm = y * 8 + lax.rem(x + 3, 4) * 2 + k
    yp = lax.rem(y + 1, 4) * 8 + x * 2 + k
    ym = lax.rem(y + 3, 4) * 8 + x * 2 + k
    xx = y * 8 + lax.rem(x + 2, 4) * 2 + k
    yy = lax.rem(y + 2, 4) * 8 + x * 2 + k

    def when(cond, act):
        if cond is True:
            act()
        else:
            pl.when(cond)(act)

    l_at = pl.multiple_of(r * 128, 128)
    loads = (
        pltpu.make_async_copy(v_hbm, v_ref, out_sem.at[0]),
        pltpu.make_async_copy(lt_hbm, lg.at[y, x, k, :, pl.ds(l_at, 128)], out_sem.at[1]),
        pltpu.make_async_copy(u_hbm, u_ref, out_sem.at[2]),
    )
    for load in loads:
        load.start()
    barrier = pltpu.get_barrier_semaphore()

    def hello(rr, cc):
        pl.semaphore_signal(barrier, inc=1, device_id=(rr, cc), device_id_type=MESH)

    for i in range(1, NZ):
        hello(lax.rem(r + i, NZ), c)
    for cc in (xp, xm, xx, yp, ym, yy, sib):
        hello(r, cc)
    for i in range(4):
        cc = 4 * r + i
        when(
            jnp.logical_not(jnp.logical_and(home == r, cc == c)),
            lambda cc=cc: hello(home, cc),
        )

    for load in loads:
        load.wait()
    lane = lax.broadcasted_iota(jnp.int32, (32, 256), 1)
    by_slot = jnp.swapaxes(v_ref[...], 0, 1)
    for s in range(8):
        width = jnp.where(s * NZ + r > k_ref[0], rank_ref[s], 0)
        kept = by_slot[s] * (lane < width).astype(jnp.bfloat16)
        js[s % 4, 0, s // 4] = kept
        vg[y, x, k, :, 256 * s : 256 * s + 256] = kept
    by_slot = jnp.swapaxes(u_ref[...], 0, 1)
    for s in range(8):
        js[s % 4, 1, s // 4] = by_slot[s]

    @pl.when(itself)
    def _():
        pl.semaphore_wait(barrier, 17)

    @pl.when(jnp.logical_not(itself))
    def _():
        pl.semaphore_wait(barrier, 18)

    def scatter(q, w):
        return pltpu.make_async_remote_copy(
            src_ref=js.at[q, w],
            dst_ref=jg.at[:, w, pl.ds(pl.multiple_of(c * 32, 32), 32)],
            send_sem=sc_s.at[w, q],
            recv_sem=sc_r.at[w, lax.rem(c, 4)],
            device_id=(spread, 8 * q + r),
            device_id_type=MESH,
        )

    def not_me(q):
        return jnp.logical_not(jnp.logical_and(spread == r, 8 * q + r == c))

    def scatter_event(w):
        for q in range(4):
            when(not_me(q), lambda: scatter(q, w).start())

            @pl.when(jnp.logical_not(not_me(q)))
            def _():
                jg[:, w, pl.ds(pl.multiple_of(c * 32, 32), 32)] = js[q, w]

    def scattered(w):
        for i in range(4):

            @pl.when(jnp.logical_not(jnp.logical_and(home == r, 4 * r + i == c)))
            def _():
                pltpu.make_async_remote_copy(
                    src_ref=js.at[0, w],
                    dst_ref=jg.at[:, w, pl.ds(pl.multiple_of((4 * r + i) * 32, 32), 32)],
                    send_sem=sc_s.at[w, 0],
                    recv_sem=sc_r.at[w, i],
                    device_id=(home, 4 * r + i),
                    device_id_type=MESH,
                ).wait_recv()

    def linv_copy(i):
        return pltpu.make_async_remote_copy(
            src_ref=lg.at[y, x, k, :, pl.ds(l_at, 128)],
            dst_ref=lg.at[y, x, k, :, pl.ds(l_at, 128)],
            send_sem=l_s.at[i - 1],
            recv_sem=l_r.at[i - 1],
            device_id=(lax.rem(r + i, NZ), c),
            device_id_type=MESH,
        )

    def linv_live(rr):
        return jnp.logical_or(y < 2, rr >= 4)

    V, L = 0, 1
    came = (-1, 1, 2)

    def at(pos, off):
        return lax.rem(pos + 4 + off, 4)

    def columns(kind, p, half=None, part=None):
        width = VW if kind == V else LW
        first = width * (p if kind == V else 1 - p)
        for cut in (part, half):
            if cut is not None:
                width //= 2
                first += width * cut
        return pl.ds(first, width)

    def near_live(kind, p, off):
        if kind == V or p == 0:
            return True
        return at(y, off) < 2

    def near(kind, p, m, off=0, half=None):
        buf = vg if kind == V else lg
        cols = columns(kind, p, half)
        to = ((xp, xm, xx), (yp, ym, yy))[p][m if kind == L else m % 2]
        if p == 0:
            ref = buf.at[y, at(x, off), k, :, cols]
        else:
            ref = buf.at[at(y, off), x, k, :, cols]
        return pltpu.make_async_remote_copy(
            src_ref=ref, dst_ref=ref,
            send_sem=v_s.at[4 if kind == L and p == 1 else 3 if kind == L else 0],
            recv_sem=near_r.at[kind, p, m],
            device_id=(r, to), device_id_type=MESH,
        )

    def group(kind, p, part, off, half=None):
        cols = columns(kind, p, half, part)
        if kind == V:
            if p == 0:
                return vg.at[at(y, off), :, k, :, cols]
            return vg.at[:, at(x, off), k, :, cols]
        if p == 0:
            return lg.at[at(y, off), :, k, :, cols]
        return lg.at[pl.ds(0, 2), at(x, off), k, :, cols]

    def far(kind, p, part, m):
        if m < 2:
            ref = group(kind, p, part, 0)
        else:
            ref = group(kind, p, part, came[m - 2], m - 2)
        to = ((yp, ym), (xp, xm))[p][m % 2]
        return pltpu.make_async_remote_copy(
            src_ref=ref, dst_ref=ref,
            send_sem=v_s.at[1 if kind == V else 3],
            recv_sem=far_r.at[kind, p, part or 0, m],
            device_id=(r, to), device_id_type=MESH,
        )

    def sibling(kind, p, part, off):
        ref = group(kind, p, part, off)
        return pltpu.make_async_remote_copy(
            src_ref=ref, dst_ref=ref,
            send_sem=v_s.at[2 if kind == V else 3],
            recv_sem=sib_r.at[kind, p, part or 0],
            device_id=(r, sib), device_id_type=MESH,
        )

    def near_start(kind, p):
        for m in (2, 0, 1) if kind == L else (0, 1):
            near(kind, p, m).start()

    def near_more(p):
        for m in range(2):
            near(V, p, m, came[m]).wait_recv()
            near(V, p, m + 2, came[m], m).start()

    def near_end(kind, p):
        if kind == V:
            for m in range(2):
                near(V, p, m + 2, 2, m).wait_recv()
        else:
            for m in range(3):
                when(
                    near_live(kind, p, came[m]),
                    lambda: near(kind, p, m, came[m]).wait_recv(),
                )

    def far_start(kind, p, part=None):
        far(kind, p, part, 0).start()
        far(kind, p, part, 1).start()
        sibling(kind, p, part, 0).start()

    def far_more(kind, p, part=None):
        for m in range(2):
            far(kind, p, part, m).wait_recv()
            far(kind, p, part, m + 2).start()
            sibling(kind, p, part, came[m]).start()

    def far_end(kind, p, part=None):
        far(kind, p, part, 2).wait_recv()
        far(kind, p, part, 3).wait_recv()
        sibling(kind, p, part, 2).start()

    def sib_got(kind, p, part=None):
        cols = columns(kind, p, None, part)
        if kind == V:
            ref = vg.at[:, :, 1 - k, :, cols]
        elif p == 0:
            ref = lg.at[:, :, 1 - k, :, cols]
        else:
            ref = lg.at[pl.ds(0, 2), :, 1 - k, :, cols]
        pltpu.make_async_remote_copy(
            src_ref=ref, dst_ref=ref, send_sem=v_s.at[2],
            recv_sem=sib_r.at[kind, p, part or 0],
            device_id=(r, sib), device_id_type=MESH,
        ).wait_recv()

    def along_z(w, d, s):
        way = 1 if d == 0 else NZ - 1
        block = lax.rem(r + s * (NZ - way), NZ)
        rows = pl.ds(pl.multiple_of(block * 128, 128), 128)
        ref = jg.at[:, w, rows] if s < 3 else jg.at[d, w, rows]
        return pltpu.make_async_remote_copy(
            src_ref=ref, dst_ref=ref,
            send_sem=z_s, recv_sem=z_r.at[w, d, s],
            device_id=(lax.rem(r + way, NZ), c), device_id_type=MESH,
        )

    def z_event(w, s):
        for d in range(2):
            if s > 0:
                along_z(w, d, s - 1).wait_recv()
            if s < 4:
                along_z(w, d, s).start()

    def solve(load, put):
        for m in range(4):
            total = None
            for n in range(m + 1):
                part = jnp.dot(
                    linv[256 * m : 256 * m + 256, 256 * n : 256 * n + 256], load(n),
                    preferred_element_type=jnp.float32,
                )
                total = part if total is None else total + part
            put(m, total.astype(jnp.bfloat16))

    def factor_turned():
        for m in range(4):
            for n in range(m + 1):
                linv[256 * m : 256 * m + 256, 256 * n : 256 * n + 256] = lg[
                    n, :, :, :, 256 * m : 256 * m + 256
                ].reshape(256, 256).T

    def columns_solved():
        def tile(t, carry):
            def put(m, block):
                sjt[t, :, 256 * m : 256 * m + 256] = block.T

            solve(lambda n: jg[t, 0, 256 * n : 256 * n + 256, :], put)
            return carry

        lax.fori_loop(0, 2, tile, 0)

    def slots(first):
        def slot(i, carry):
            s = first + i
            cols = pl.ds(pl.multiple_of(s * 256, 256), 256)

            def put(m, block):
                sa[s, 256 * m : 256 * m + 256, :] = block

            solve(lambda n: vg[n, :, :, :, cols].reshape(256, 256), put)
            solved_out[s] = sa[s, pl.ds(pl.multiple_of(c * 32, 32), 32), :]
            return carry

        lax.fori_loop(0, 2, slot, 0)

    def cores(first, count):
        def slot(i, carry):
            s = first + i
            for t in range(2):

                @pl.when(c + 32 * t <= s * NZ + r)
                def _():
                    core[s, t] = jnp.dot(
                        sjt[t], sa[s], preferred_element_type=jnp.float32
                    ).astype(jnp.bfloat16)

            core_copy(s).start()
            return carry

        lax.fori_loop(0, count, slot, 0)

    def core_copy(s):
        return pltpu.make_async_copy(core.at[s], core_out.at[s], core_s.at[s])

    for i in (4, 3, 5, 2, 6, 1, 7):
        when(linv_live(r), lambda: linv_copy(i).start())
    scatter_event(0)
    near_start(V, 0)
    near_start(V, 1)
    scatter_event(1)
    for i in range(1, NZ):
        when(linv_live(lax.rem(r + NZ - i, NZ)), lambda: linv_copy(i).wait_recv())
    near_start(L, 0)
    when(near_live(L, 1, 0), lambda: near_start(L, 1))
    scattered(0)
    z_event(0, 0)
    near_more(0)
    near_more(1)
    scattered(1)
    z_event(1, 0)
    for p in (1, 0):
        near_end(L, p)
        far_start(L, p)
    z_event(0, 1)
    for p in (1, 0):
        near_end(V, p)
        far_start(V, p, 0)
    z_event(1, 1)
    far_more(L, 1)
    far_start(V, 1, 1)
    z_event(0, 2)
    far_more(L, 0)
    far_start(V, 0, 1)
    far_more(V, 1, 0)
    far_end(L, 1)
    z_event(1, 2)
    far_more(V, 0, 0)
    far_more(V, 1, 1)
    far_end(L, 0)
    z_event(0, 3)
    far_end(V, 1, 0)
    far_more(V, 0, 1)
    sib_got(L, 1)
    sib_got(L, 0)
    factor_turned()
    z_event(1, 3)
    far_end(V, 1, 1)
    far_end(V, 0, 0)
    sib_got(V, 1, 0)
    slots(4)
    far_end(V, 0, 1)
    sib_got(V, 0, 0)
    slots(0)
    z_event(0, 4)
    columns_solved()
    cores(4, 2)
    cores(0, 2)
    z_event(1, 4)
    out_u = pltpu.make_async_copy(jg.at[:, 1], u_out, out_sem.at[1])
    out_u.start()
    sib_got(V, 1, 1)
    slots(6)
    cores(6, 2)
    sib_got(V, 0, 1)
    slots(2)
    cores(2, 2)

    def all_sent(sem, ref):
        pltpu.make_async_remote_copy(
            src_ref=ref, dst_ref=ref, send_sem=sem, recv_sem=l_r.at[0],
            device_id=(r, sib), device_id_type=MESH,
        ).wait_send()

    for sem, rows in (
        (v_s.at[0], 192), (v_s.at[1], 768), (v_s.at[2], 1024), (v_s.at[3], 720), (z_s, 896),
    ):
        all_sent(sem, linv.at[pl.ds(0, rows)])
    when(
        near_live(L, 1, 0),
        lambda: all_sent(v_s.at[4], linv.at[pl.ds(0, 48)]),
    )
    for i in range(1, NZ):
        when(linv_live(r), lambda: linv_copy(i).wait_send())
    for w in range(2):
        for q in range(4):
            when(not_me(q), lambda: scatter(q, w).wait_send())
    for s in range(8):
        core_copy(s).wait()
    out_u.wait()


def gather(ranks, panel_index, tile_u, tile_v, inverse_factor):
    dma = pltpu.SemaphoreType.DMA
    bf16 = jnp.bfloat16
    vmem = pl.BlockSpec(memory_space=pltpu.VMEM)
    smem = pl.BlockSpec(memory_space=pltpu.SMEM)
    hbm = pl.BlockSpec(memory_space=pl.ANY)
    return pl.pallas_call(
        gather_kernel,
        out_shape=(
            jax.ShapeDtypeStruct((8, 2, 256, 256), bf16),
            jax.ShapeDtypeStruct((2, 1024, 256), bf16),
            jax.ShapeDtypeStruct((8, 32, 256), bf16),
        ),
        in_specs=[smem, smem, hbm, hbm, hbm],
        out_specs=[hbm, hbm, vmem],
        scratch_shapes=[
            pltpu.VMEM((32, 8, 256), bf16),
            pltpu.VMEM((32, 8, 256), bf16),
            pltpu.VMEM((4, 2, 2, 32, 256), bf16),
            pltpu.VMEM((NY, NX, 2, 32, 2 * VW), bf16),
            pltpu.VMEM((NY, NX, 2, 32, 2 * LW), bf16),
            pltpu.VMEM((2, 2, 1024, 256), bf16),
            pltpu.VMEM((1024, 1024), bf16),
            pltpu.VMEM((2, 256, 1024), bf16),
            pltpu.VMEM((8, 1024, 256), bf16),
            pltpu.VMEM((8, 2, 256, 256), bf16),
            dma((2, 4)), dma((2, 4)),
            dma((7,)), dma((7,)),
            dma((2, 2, 4)), dma((2, 2, 2, 4)), dma((2, 2, 2)),
            dma, dma((2, 2, 4)),
            dma((5,)), dma((3,)), dma((8,)),
        ],
        compiler_params=pltpu.CompilerParams(
            collective_id=0, has_side_effects=True, vmem_limit_bytes=60 * 2**20
        ),
        name="gather",
    )(ranks, panel_index, tile_u, tile_v, inverse_factor)


def update_kernel(
    k_ref, core_hbm, u_hbm, solved_ref, out_ref, solved_out,
    core_ref, u_ref, zero, block, sem, core_sem, u_sem,
):
    r = lax.axis_index("row")
    c = lax.axis_index("col")

    def is_live(s, t):
        col_tile = c + 32 * t
        return jnp.logical_and(col_tile > k_ref[0], col_tile <= s * NZ + r)

    def send(src, s, t):
        return pltpu.make_async_copy(src, out_ref.at[s, t], sem.at[s, t])

    def core_load(s):
        return pltpu.make_async_copy(core_hbm.at[s], core_ref.at[s], core_sem.at[s])

    def u_load(t):
        return pltpu.make_async_copy(u_hbm.at[t], u_ref.at[t], u_sem.at[t])

    u_load(0).start()
    core_load(0).start()
    u_load(1).start()
    for s in range(1, 8):
        core_load(s).start()
    zero[...] = jnp.zeros((1024, 256), jnp.bfloat16)

    def dead(s, carry):
        for t in range(2):

            @pl.when(jnp.logical_not(is_live(s, t)))
            def _():
                send(zero, s, t).start()

        return carry

    def live(t):
        u_load(t).wait()

        def slot(s, carry):
            if t == 0:
                core_load(s).wait()

            @pl.when(is_live(s, t))
            def _():
                block[s, t] = jnp.dot(
                    u_ref[t], core_ref[s, t], preferred_element_type=jnp.float32
                ).astype(jnp.bfloat16)
                send(block.at[s, t], s, t).start()

            return carry

        lax.fori_loop(0, 8, slot, 0)

    def done(s, carry):
        for t in range(2):
            send(block.at[s, t], s, t).wait()
        return carry

    lax.fori_loop(0, 8, dead, 0)
    live(0)
    live(1)
    solved_out[...] = jnp.swapaxes(solved_ref[...], 0, 1)
    lax.fori_loop(0, 8, done, 0)


def update(panel_index, core, column_u, solved):
    vmem = pl.BlockSpec(memory_space=pltpu.VMEM)
    hbm = pl.BlockSpec(memory_space=pl.ANY)
    return pl.pallas_call(
        update_kernel,
        out_shape=(
            jax.ShapeDtypeStruct((8, 2, 1024, 256), jnp.bfloat16),
            jax.ShapeDtypeStruct((32, 8, 256), jnp.bfloat16),
        ),
        in_specs=[pl.BlockSpec(memory_space=pltpu.SMEM), hbm, hbm, vmem],
        out_specs=[hbm, vmem],
        scratch_shapes=[
            pltpu.VMEM((8, 2, 256, 256), jnp.bfloat16),
            pltpu.VMEM((2, 1024, 256), jnp.bfloat16),
            pltpu.VMEM((1024, 256), jnp.bfloat16),
            pltpu.VMEM((8, 2, 1024, 256), jnp.bfloat16),
            pltpu.SemaphoreType.DMA((8, 2)),
            pltpu.SemaphoreType.DMA((8,)),
            pltpu.SemaphoreType.DMA((2,)),
        ],
        compiler_params=pltpu.CompilerParams(vmem_limit_bytes=60 * 2**20),
        name="update",
    )(panel_index, core, column_u, solved)


def per_device(tile_u, tile_v, inverse_factor, ranks, panel_index):
    core, column_u, solved = gather(ranks, panel_index, tile_u, tile_v, inverse_factor.T)
    return update(panel_index, core, column_u, solved)


def solution(mesh):
    placed = (P("col", "row", None), P("col", "row", None), P("row", "col"), P("row"), P())
    return jax.shard_map(
        per_device,
        mesh=mesh,
        in_specs=placed,
        out_specs=(P("row", "col", None, None), P("col", "row", None)),
        check_vma=False,
    )
```

```python
import jax
import jax.numpy as jnp
from jax import lax
from jax.experimental import pallas as pl
from jax.experimental.pallas import tpu as pltpu
from jax.sharding import PartitionSpec as P

MESH = pl.DeviceIdType.MESH
NZ = 8
NX = 4
NY = 4
VW = 1024
LW = 512


def dev(r, c):
    return (r, c)


def gather_kernel(
    rank_ref, k_ref, u_hbm, v_hbm, lt_hbm, core_out, u_out, solved_out,
    u_ref, v_ref, js, vg, lg, jg, linv, sjt, sa, core,
    sc_s, sc_r, l_s, l_r, near_r, far_r, sib_r, across_r, z_s, z_r, v_s, out_sem, core_s,
):
    r = lax.axis_index("row")
    c = lax.axis_index("col")
    y = lax.div(c, 8)
    x = lax.rem(lax.div(c, 2), 4)
    k = lax.rem(c, 2)
    sib = c + 1 - 2 * k
    home = lax.rem(c, 8)
    spread = lax.div(c, 4)
    itself = jnp.logical_and(spread == r, home == r)
    xp = y * 8 + lax.rem(x + 1, 4) * 2 + k
    xm = y * 8 + lax.rem(x + 3, 4) * 2 + k
    yp = lax.rem(y + 1, 4) * 8 + x * 2 + k
    ym = lax.rem(y + 3, 4) * 8 + x * 2 + k
    xx = y * 8 + lax.rem(x + 2, 4) * 2 + k
    yy = lax.rem(y + 2, 4) * 8 + x * 2 + k

    def when(cond, act):
        if cond is True:
            act()
        else:
            pl.when(cond)(act)

    l_at = pl.multiple_of(r * 128, 128)
    loads = (
        pltpu.make_async_copy(v_hbm, v_ref, out_sem.at[0]),
        pltpu.make_async_copy(lt_hbm, lg.at[y, x, k, :, pl.ds(l_at, 128)], out_sem.at[1]),
        pltpu.make_async_copy(u_hbm, u_ref, out_sem.at[2]),
    )
    for load in loads:
        load.start()
    barrier = pltpu.get_barrier_semaphore()

    def hello(rr, cc):
        pl.semaphore_signal(barrier, inc=1, device_id=(rr, cc), device_id_type=MESH)

    for i in range(1, NZ):
        hello(lax.rem(r + i, NZ), c)
    for cc in (xp, xm, xx, yp, ym, yy, sib):
        hello(r, cc)
    for cc in (xp, xm, yp, ym):
        hello(r, cc + 1 - 2 * k)
    for i in range(4):
        cc = 4 * r + i
        when(
            jnp.logical_not(jnp.logical_and(home == r, cc == c)),
            lambda cc=cc: hello(home, cc),
        )

    for load in loads:
        load.wait()
    lane = lax.broadcasted_iota(jnp.int32, (32, 256), 1)
    by_slot = jnp.swapaxes(v_ref[...], 0, 1)
    for s in range(8):
        width = jnp.where(s * NZ + r > k_ref[0], rank_ref[s], 0)
        kept = by_slot[s] * (lane < width).astype(jnp.bfloat16)
        js[s % 4, 0, s // 4] = kept
        vg[y, x, k, :, 256 * s : 256 * s + 256] = kept
    by_slot = jnp.swapaxes(u_ref[...], 0, 1)
    for s in range(8):
        js[s % 4, 1, s // 4] = by_slot[s]

    @pl.when(itself)
    def _():
        pl.semaphore_wait(barrier, 21)

    @pl.when(jnp.logical_not(itself))
    def _():
        pl.semaphore_wait(barrier, 22)

    def scatter(q, w):
        return pltpu.make_async_remote_copy(
            src_ref=js.at[q, w],
            dst_ref=jg.at[:, w, pl.ds(pl.multiple_of(c * 32, 32), 32)],
            send_sem=sc_s.at[w, q],
            recv_sem=sc_r.at[w, lax.rem(c, 4)],
            device_id=(spread, 8 * q + r),
            device_id_type=MESH,
        )

    def not_me(q):
        return jnp.logical_not(jnp.logical_and(spread == r, 8 * q + r == c))

    def scatter_event(w):
        for q in range(4):
            when(not_me(q), lambda: scatter(q, w).start())

            @pl.when(jnp.logical_not(not_me(q)))
            def _():
                jg[:, w, pl.ds(pl.multiple_of(c * 32, 32), 32)] = js[q, w]

    def scattered(w):
        for i in range(4):

            @pl.when(jnp.logical_not(jnp.logical_and(home == r, 4 * r + i == c)))
            def _():
                pltpu.make_async_remote_copy(
                    src_ref=js.at[0, w],
                    dst_ref=jg.at[:, w, pl.ds(pl.multiple_of((4 * r + i) * 32, 32), 32)],
                    send_sem=sc_s.at[w, 0],
                    recv_sem=sc_r.at[w, i],
                    device_id=(home, 4 * r + i),
                    device_id_type=MESH,
                ).wait_recv()

    def linv_copy(i):
        return pltpu.make_async_remote_copy(
            src_ref=lg.at[y, x, k, :, pl.ds(l_at, 128)],
            dst_ref=lg.at[y, x, k, :, pl.ds(l_at, 128)],
            send_sem=l_s.at[i - 1],
            recv_sem=l_r.at[i - 1],
            device_id=(lax.rem(r + i, NZ), c),
            device_id_type=MESH,
        )

    def linv_live(rr):
        return jnp.logical_or(y < 2, rr >= 4)

    V, L = 0, 1
    came = (-1, 1, 2)

    def at(pos, off):
        return lax.rem(pos + 4 + off, 4)

    def columns(kind, p, half=None, part=None):
        width = VW if kind == V else LW
        first = width * (p if kind == V else 1 - p)
        for cut in (part, half):
            if cut is not None:
                width //= 2
                first += width * cut
        return pl.ds(first, width)

    def near_live(kind, p, off):
        if kind == V or p == 0:
            return True
        return at(y, off) < 2

    def near(kind, p, m, off=0, half=None):
        buf = vg if kind == V else lg
        cols = columns(kind, p, half)
        to = ((xp, xm, xx), (yp, ym, yy))[p][m if kind == L else m % 2]
        if p == 0:
            ref = buf.at[y, at(x, off), k, :, cols]
        else:
            ref = buf.at[at(y, off), x, k, :, cols]
        return pltpu.make_async_remote_copy(
            src_ref=ref, dst_ref=ref,
            send_sem=v_s.at[4 if kind == L and p == 1 else 3 if kind == L else 0],
            recv_sem=near_r.at[kind, p, m],
            device_id=(r, to), device_id_type=MESH,
        )

    def group(kind, p, part, off, half=None):
        cols = columns(kind, p, half, part)
        if kind == V:
            if p == 0:
                return vg.at[at(y, off), :, k, :, cols]
            return vg.at[:, at(x, off), k, :, cols]
        if p == 0:
            return lg.at[at(y, off), :, k, :, cols]
        return lg.at[pl.ds(0, 2), at(x, off), k, :, cols]

    def far(kind, p, part, m):
        if m < 2:
            ref = group(kind, p, part, 0)
        else:
            ref = group(kind, p, part, came[m - 2], m - 2)
        to = ((yp, ym), (xp, xm))[p][m % 2]
        return pltpu.make_async_remote_copy(
            src_ref=ref, dst_ref=ref,
            send_sem=v_s.at[1 if kind == V else 3],
            recv_sem=far_r.at[kind, p, part or 0, m],
            device_id=(r, to), device_id_type=MESH,
        )

    def across(p, part, m):
        ref = group(V, p, part, came[m - 2], m - 2)
        to = ((yp, ym), (xp, xm))[p][m % 2] + 1 - 2 * k
        return pltpu.make_async_remote_copy(
            src_ref=ref, dst_ref=ref,
            send_sem=v_s.at[1], recv_sem=across_r.at[p, part, m - 2],
            device_id=(r, to), device_id_type=MESH,
        )

    def sibling(kind, p, part, off):
        ref = group(kind, p, part, off)
        return pltpu.make_async_remote_copy(
            src_ref=ref, dst_ref=ref,
            send_sem=v_s.at[2 if kind == V else 3],
            recv_sem=sib_r.at[kind, p, part or 0],
            device_id=(r, sib), device_id_type=MESH,
        )

    def near_start(kind, p):
        for m in (2, 0, 1) if kind == L else (0, 1):
            near(kind, p, m).start()

    def near_more(p):
        for m in range(2):
            near(V, p, m, came[m]).wait_recv()
            near(V, p, m + 2, came[m], m).start()

    def near_end(kind, p):
        if kind == V:
            for m in range(2):
                near(V, p, m + 2, 2, m).wait_recv()
        else:
            for m in range(3):
                when(
                    near_live(kind, p, came[m]),
                    lambda: near(kind, p, m, came[m]).wait_recv(),
                )

    def far_start(kind, p, part=None):
        far(kind, p, part, 0).start()
        far(kind, p, part, 1).start()
        sibling(kind, p, part, 0).start()

    def far_more(kind, p, part=None):
        for m in range(2):
            far(kind, p, part, m).wait_recv()
            far(kind, p, part, m + 2).start()
            if kind == V:
                across(p, part, m + 2).start()
            sibling(kind, p, part, came[m]).start()

    def far_end(kind, p, part=None):
        far(kind, p, part, 2).wait_recv()
        far(kind, p, part, 3).wait_recv()
        if kind == L:
            sibling(kind, p, part, 2).start()

    def sib_got(kind, p, part=None):
        cols = columns(kind, p, None, part)
        if kind == V:
            if p == 0:
                ref = vg.at[pl.ds(0, 3), :, 1 - k, :, cols]
            else:
                ref = vg.at[:, pl.ds(0, 3), 1 - k, :, cols]
            across(p, part, 2).wait_recv()
            across(p, part, 3).wait_recv()
        elif p == 0:
            ref = lg.at[:, :, 1 - k, :, cols]
        else:
            ref = lg.at[pl.ds(0, 2), :, 1 - k, :, cols]
        pltpu.make_async_remote_copy(
            src_ref=ref, dst_ref=ref, send_sem=v_s.at[2],
            recv_sem=sib_r.at[kind, p, part or 0],
            device_id=(r, sib), device_id_type=MESH,
        ).wait_recv()

    def along_z(w, d, s):
        way = 1 if d == 0 else NZ - 1
        block = lax.rem(r + s * (NZ - way), NZ)
        rows = pl.ds(pl.multiple_of(block * 128, 128), 128)
        ref = jg.at[:, w, rows] if s < 3 else jg.at[d, w, rows]
        return pltpu.make_async_remote_copy(
            src_ref=ref, dst_ref=ref,
            send_sem=z_s, recv_sem=z_r.at[w, d, s],
            device_id=(lax.rem(r + way, NZ), c), device_id_type=MESH,
        )

    def z_event(w, s):
        for d in range(2):
            if s > 0:
                along_z(w, d, s - 1).wait_recv()
            if s < 4:
                along_z(w, d, s).start()

    def solve(load, put):
        for m in range(4):
            total = None
            for n in range(m + 1):
                part = jnp.dot(
                    linv[256 * m : 256 * m + 256, 256 * n : 256 * n + 256], load(n),
                    preferred_element_type=jnp.float32,
                )
                total = part if total is None else total + part
            put(m, total.astype(jnp.bfloat16))

    def factor_turned():
        for m in range(4):
            for n in range(m + 1):
                linv[256 * m : 256 * m + 256, 256 * n : 256 * n + 256] = lg[
                    n, :, :, :, 256 * m : 256 * m + 256
                ].reshape(256, 256).T

    def columns_solved():
        def tile(t, carry):
            def put(m, block):
                sjt[t, :, 256 * m : 256 * m + 256] = block.T

            solve(lambda n: jg[t, 0, 256 * n : 256 * n + 256, :], put)
            return carry

        lax.fori_loop(0, 2, tile, 0)

    def slots(first):
        def slot(i, carry):
            s = first + i
            cols = pl.ds(pl.multiple_of(s * 256, 256), 256)

            def put(m, block):
                sa[s, 256 * m : 256 * m + 256, :] = block

            solve(lambda n: vg[n, :, :, :, cols].reshape(256, 256), put)
            solved_out[s] = sa[s, pl.ds(pl.multiple_of(c * 32, 32), 32), :]
            return carry

        lax.fori_loop(0, 2, slot, 0)

    def cores(first, count):
        def slot(i, carry):
            s = first + i
            for t in range(2):

                @pl.when(c + 32 * t <= s * NZ + r)
                def _():
                    core[s, t] = jnp.dot(
                        sjt[t], sa[s], preferred_element_type=jnp.float32
                    ).astype(jnp.bfloat16)

            core_copy(s).start()
            return carry

        lax.fori_loop(0, count, slot, 0)

    def core_copy(s):
        return pltpu.make_async_copy(core.at[s], core_out.at[s], core_s.at[s])

    for i in (4, 3, 5, 2, 6, 1, 7):
        when(linv_live(r), lambda: linv_copy(i).start())
    scatter_event(0)
    near_start(V, 0)
    near_start(V, 1)
    scatter_event(1)
    for i in range(1, NZ):
        when(linv_live(lax.rem(r + NZ - i, NZ)), lambda: linv_copy(i).wait_recv())
    near_start(L, 0)
    when(near_live(L, 1, 0), lambda: near_start(L, 1))
    scattered(0)
    z_event(0, 0)
    near_more(0)
    near_more(1)
    scattered(1)
    z_event(1, 0)
    for p in (1, 0):
        near_end(L, p)
        far_start(L, p)
    z_event(0, 1)
    for p in (1, 0):
        near_end(V, p)
        far_start(V, p, 0)
    z_event(1, 1)
    far_more(L, 1)
    far_start(V, 1, 1)
    z_event(0, 2)
    far_more(L, 0)
    far_start(V, 0, 1)
    far_more(V, 1, 0)
    far_end(L, 1)
    z_event(1, 2)
    far_more(V, 0, 0)
    far_more(V, 1, 1)
    far_end(L, 0)
    z_event(0, 3)
    far_end(V, 1, 0)
    far_more(V, 0, 1)
    sib_got(L, 1)
    sib_got(L, 0)
    factor_turned()
    z_event(1, 3)
    far_end(V, 1, 1)
    far_end(V, 0, 0)
    sib_got(V, 1, 0)
    slots(4)
    far_end(V, 0, 1)
    sib_got(V, 0, 0)
    slots(0)
    z_event(0, 4)
    columns_solved()
    cores(4, 2)
    cores(0, 2)
    z_event(1, 4)
    out_u = pltpu.make_async_copy(jg.at[:, 1], u_out, out_sem.at[1])
    out_u.start()
    sib_got(V, 1, 1)
    slots(6)
    cores(6, 2)
    sib_got(V, 0, 1)
    slots(2)
    cores(2, 2)

    def all_sent(sem, ref):
        pltpu.make_async_remote_copy(
            src_ref=ref, dst_ref=ref, send_sem=sem, recv_sem=l_r.at[0],
            device_id=(r, sib), device_id_type=MESH,
        ).wait_send()

    for sem, rows in (
        (v_s.at[0], 192), (v_s.at[1], 1024), (v_s.at[2], 768), (v_s.at[3], 720), (z_s, 896),
    ):
        all_sent(sem, linv.at[pl.ds(0, rows)])
    when(
        near_live(L, 1, 0),
        lambda: all_sent(v_s.at[4], linv.at[pl.ds(0, 48)]),
    )
    for i in range(1, NZ):
        when(linv_live(r), lambda: linv_copy(i).wait_send())
    for w in range(2):
        for q in range(4):
            when(not_me(q), lambda: scatter(q, w).wait_send())
    for s in range(8):
        core_copy(s).wait()
    out_u.wait()


def gather(ranks, panel_index, tile_u, tile_v, inverse_factor):
    dma = pltpu.SemaphoreType.DMA
    bf16 = jnp.bfloat16
    vmem = pl.BlockSpec(memory_space=pltpu.VMEM)
    smem = pl.BlockSpec(memory_space=pltpu.SMEM)
    hbm = pl.BlockSpec(memory_space=pl.ANY)
    return pl.pallas_call(
        gather_kernel,
        out_shape=(
            jax.ShapeDtypeStruct((8, 2, 256, 256), bf16),
            jax.ShapeDtypeStruct((2, 1024, 256), bf16),
            jax.ShapeDtypeStruct((8, 32, 256), bf16),
        ),
        in_specs=[smem, smem, hbm, hbm, hbm],
        out_specs=[hbm, hbm, vmem],
        scratch_shapes=[
            pltpu.VMEM((32, 8, 256), bf16),
            pltpu.VMEM((32, 8, 256), bf16),
            pltpu.VMEM((4, 2, 2, 32, 256), bf16),
            pltpu.VMEM((NY, NX, 2, 32, 2 * VW), bf16),
            pltpu.VMEM((NY, NX, 2, 32, 2 * LW), bf16),
            pltpu.VMEM((2, 2, 1024, 256), bf16),
            pltpu.VMEM((1024, 1024), bf16),
            pltpu.VMEM((2, 256, 1024), bf16),
            pltpu.VMEM((8, 1024, 256), bf16),
            pltpu.VMEM((8, 2, 256, 256), bf16),
            dma((2, 4)), dma((2, 4)),
            dma((7,)), dma((7,)),
            dma((2, 2, 4)), dma((2, 2, 2, 4)), dma((2, 2, 2)),
            dma((2, 2, 2)),
            dma, dma((2, 2, 4)),
            dma((5,)), dma((3,)), dma((8,)),
        ],
        compiler_params=pltpu.CompilerParams(
            collective_id=0, has_side_effects=True, vmem_limit_bytes=60 * 2**20
        ),
        name="gather",
    )(ranks, panel_index, tile_u, tile_v, inverse_factor)


def update_kernel(
    k_ref, core_hbm, u_hbm, solved_ref, out_ref, solved_out,
    core_ref, u_ref, zero, block, sem, core_sem, u_sem,
):
    r = lax.axis_index("row")
    c = lax.axis_index("col")

    def is_live(s, t):
        col_tile = c + 32 * t
        return jnp.logical_and(col_tile > k_ref[0], col_tile <= s * NZ + r)

    def send(src, s, t):
        return pltpu.make_async_copy(src, out_ref.at[s, t], sem.at[s, t])

    def core_load(s):
        return pltpu.make_async_copy(core_hbm.at[s], core_ref.at[s], core_sem.at[s])

    def u_load(t):
        return pltpu.make_async_copy(u_hbm.at[t], u_ref.at[t], u_sem.at[t])

    u_load(0).start()
    core_load(0).start()
    u_load(1).start()
    for s in range(1, 8):
        core_load(s).start()
    zero[...] = jnp.zeros((1024, 256), jnp.bfloat16)

    def dead(s, carry):
        for t in range(2):

            @pl.when(jnp.logical_not(is_live(s, t)))
            def _():
                send(zero, s, t).start()

        return carry

    def live(t):
        u_load(t).wait()

        def slot(s, carry):
            if t == 0:
                core_load(s).wait()

            @pl.when(is_live(s, t))
            def _():
                block[s, t] = jnp.dot(
                    u_ref[t], core_ref[s, t], preferred_element_type=jnp.float32
                ).astype(jnp.bfloat16)
                send(block.at[s, t], s, t).start()

            return carry

        lax.fori_loop(0, 8, slot, 0)

    def done(s, carry):
        for t in range(2):
            send(block.at[s, t], s, t).wait()
        return carry

    lax.fori_loop(0, 8, dead, 0)
    live(0)
    live(1)
    solved_out[...] = jnp.swapaxes(solved_ref[...], 0, 1)
    lax.fori_loop(0, 8, done, 0)


def update(panel_index, core, column_u, solved):
    vmem = pl.BlockSpec(memory_space=pltpu.VMEM)
    hbm = pl.BlockSpec(memory_space=pl.ANY)
    return pl.pallas_call(
        update_kernel,
        out_shape=(
            jax.ShapeDtypeStruct((8, 2, 1024, 256), jnp.bfloat16),
            jax.ShapeDtypeStruct((32, 8, 256), jnp.bfloat16),
        ),
        in_specs=[pl.BlockSpec(memory_space=pltpu.SMEM), hbm, hbm, vmem],
        out_specs=[hbm, vmem],
        scratch_shapes=[
            pltpu.VMEM((8, 2, 256, 256), jnp.bfloat16),
            pltpu.VMEM((2, 1024, 256), jnp.bfloat16),
            pltpu.VMEM((1024, 256), jnp.bfloat16),
            pltpu.VMEM((8, 2, 1024, 256), jnp.bfloat16),
            pltpu.SemaphoreType.DMA((8, 2)),
            pltpu.SemaphoreType.DMA((8,)),
            pltpu.SemaphoreType.DMA((2,)),
        ],
        compiler_params=pltpu.CompilerParams(vmem_limit_bytes=60 * 2**20),
        name="update",
    )(panel_index, core, column_u, solved)


def per_device(tile_u, tile_v, inverse_factor, ranks, panel_index):
    core, column_u, solved = gather(ranks, panel_index, tile_u, tile_v, inverse_factor.T)
    return update(panel_index, core, column_u, solved)


def solution(mesh):
    placed = (P("col", "row", None), P("col", "row", None), P("row", "col"), P("row"), P())
    return jax.shard_map(
        per_device,
        mesh=mesh,
        in_specs=placed,
        out_specs=(P("row", "col", None, None), P("col", "row", None)),
        check_vma=False,
    )
```
